32 devices in a mesh: con: 4 (over z), grid: 8 (over y, x, core).
Axes of the slice: x: 2, y: 2, z: 4, core: 2. Of those that a mesh axis runs over, the one named last changes fastest.
Arguments:
- velocity: bfloat16 [8, 2, 512, 512], P('con', None, 'grid'), may hold values from -6 to 6
- seed_adjoint: bfloat16 [8, 2, 512, 512], P('con', None, 'grid'), may hold values from -6 to 6
- land_mask: int32 [512, 512], P('grid'), may hold values from 0 to 2
- inv_x: bfloat16 [4, 128, 128], replicated, may hold values from -0.5 to 0.5
- inv_y: bfloat16 [4, 128, 128], replicated, may hold values from -0.5 to 0.5
- weights: float32 [8], P('con'), may hold values from 0.05 to 0.5
Outputs:
- velocity_adjoint: float32 [8, 2, 512, 512], P('con', None, 'grid')
The draws below stay inside these ranges and needn't reach their ends.
Inputs may be any that keep to these rules, and one draw needn't show every extreme that they name: `land_mask`: 0 marks land, 1 a wet interior cell, 2 an open-boundary cell whose value is prescribed.
All inputs are finite; a program needn't handle non-finite values.
Results may differ from the reference program's by a relative error of at most 0.0039.
Values may be sent and summed in bfloat16 or wider, within the bound.
A program may use at most 64 MiB of HBM per device.

```python
import math
import jax
import jax.numpy as jnp
from jax import lax

C = 8
BLK = 128
SIDE = 512
NBLK = 4


def with_ends(entries, own_key, low, top_value):
    longest = entries.shape.index(max(entries.shape))
    spots = []
    for shift in (0, 1):
        where = [jax.random.randint(jax.random.fold_in(own_key, axis), (), 0, length) for axis, length in enumerate(entries.shape)]
        where[longest] = (where[longest] + shift) % entries.shape[longest]
        spots.append(tuple(where))
    return entries.at[spots[0]].set(low).at[spots[1]].set(top_value)


def block_scale(stream_key, extent, shards, least, high):
    level = 1.0
    for dim, shards_of in shards:
        steps = jax.random.uniform(jax.random.fold_in(jax.random.fold_in(stream_key, 6), dim), (shards_of,), jnp.float32, least / len(shards), high / len(shards))
        level = level * jnp.repeat(jnp.exp(steps), extent[dim] // shards_of).reshape((-1,) + (1,) * (len(extent) - 1 - dim))
    return level


def noise(rng, dims, scale, reach, split=(), held_as=jnp.bfloat16):
    array = scale * jax.random.normal(rng, dims, jnp.float32)
    if split:
        array = array * block_scale(rng, dims, split, -0.22, 0.18)
    return jnp.clip(array, -reach, reach).astype(held_as)


def setup_inputs(seed: int = 0) -> dict:
    key_of = jax.random.split(jax.random.key(seed), 7)
    velocity = noise(key_of[0], (C, 2, SIDE, SIDE), 1.0, 6.0, ((0, 4), (2, 8)))
    seed_adjoint = noise(key_of[1], (C, 2, SIDE, SIDE), 1.0, 6.0, ((0, 4), (2, 8)))
    land_mask = with_ends(jax.random.randint(key_of[2], (SIDE, SIDE), 0, 3), jax.random.fold_in(key_of[2], 1), 0, 2).astype(jnp.int32)
    inv_x = noise(key_of[3], (NBLK, BLK, BLK), BLK ** -0.5, 0.5)
    inv_y = noise(key_of[4], (NBLK, BLK, BLK), BLK ** -0.5, 0.5)
    weights = jnp.clip(jnp.exp(math.log(0.5) - 2.3025851 * jax.random.uniform(key_of[5], (C,), jnp.float32) ** block_scale(key_of[5], (C,), ((0, 4),), -0.2, 0.2)), 0.05, 0.5)
    return dict(velocity=velocity, seed_adjoint=seed_adjoint, land_mask=land_mask, inv_x=inv_x, inv_y=inv_y, weights=weights)


def solve_blocks(field, inverse):
    shape = field.shape
    blocks = field.astype(jnp.float32).reshape(shape[:-1] + (NBLK, BLK))
    result = jnp.einsum('pyki,kji->pykj', blocks, inverse.astype(jnp.float32))
    return result.reshape(shape)

def reference(velocity, seed_adjoint, land_mask, inv_x, inv_y, weights):
    sea = (land_mask == 1).astype(jnp.float32)
    sea_half = sea.astype(jnp.bfloat16)
    squares = jnp.zeros((SIDE, SIDE), jnp.float32)
    for con_index in range(C):
        vel = velocity[con_index].astype(jnp.float32)
        squares = squares + weights[con_index] * lax.optimization_barrier(jnp.sum(vel * vel, axis=0))
    speed = jnp.sqrt(0.25 + squares)
    inner = jnp.zeros((SIDE, SIDE), jnp.float32)
    solved = []
    for con_index in range(C):
        across = solve_blocks(seed_adjoint[con_index], inv_x).astype(jnp.bfloat16)
        masked = jnp.swapaxes(across, 1, 2) * sea_half[None]
        rows = solve_blocks(masked, inv_y)
        solved.append(rows)
        inner = inner + lax.optimization_barrier(jnp.sum(rows * velocity[con_index].astype(jnp.float32), axis=0))
    results = []
    for con_index in range(C):
        vel = velocity[con_index].astype(jnp.float32)
        term = -0.5 * sea * speed * solved[con_index] - 0.5 * sea * weights[con_index] * vel * inner / speed
        results.append(term)
    return jnp.stack(results, axis=0)
```

```python
import functools
import jax
import jax.numpy as jnp
from jax import lax
from jax.experimental import pallas as pl
from jax.experimental.pallas import tpu as pltpu
from jax.sharding import PartitionSpec as P

BLK = 128
MESH = pl.DeviceIdType.MESH
F32, BF16 = jnp.float32, jnp.bfloat16
LAST = (((1,), (1,)), ((), ()))


def partner(own, step, count):
    if count & (count - 1):
        return lax.rem(own + step, count)
    total, bit = 0, 1
    while bit < count:
        mine = lax.rem(lax.div(own, bit), 2)
        turn = step // bit % 2 if isinstance(step, int) else lax.rem(lax.div(step, bit), 2)
        total = total + lax.rem(mine + turn, 2) * bit
        bit *= 2
    return total


def steps(first, stop, body):
    if stop - first <= 8:
        for step in range(first, stop):
            body(step)
    else:
        @pl.loop(first, stop)
        def _(step):
            body(step)


def lanes(block):
    return pl.ds(pl.multiple_of(block * BLK, BLK), BLK)


def kernel(
    dims,
    vel_hbm, seed_hbm, land_hbm, ix_hbm, iy_hbm, w_ref,
    out_ref,
    vel, seed, land, ix, iy,
    send, recv, wide, mask,
    sq_part, sq_send, sq_rs, sq_ag,
    rhs, in_part, in_send, in_rs, in_ag, ca, cb,
    load_sem, a2a_send, a2a_recv, sq_send_sem, sq_recv_sem, in_send_sem, in_recv_sem,
):
    n_con, n_grid, n_blk, con_local, rows, side = dims
    pack = BLK // rows
    n_cp = con_local * 2
    groups = n_cp // pack
    share = rows // n_con
    me = lax.axis_index("grid")
    zc = lax.axis_index("con")
    own = lax.div(me, pack)
    core = lax.rem(me, pack)

    loads = []
    for i, (src, dst) in enumerate(((seed_hbm, seed), (ix_hbm, ix), (vel_hbm, vel), (iy_hbm, iy), (land_hbm, land))):
        copy = pltpu.make_async_copy(src, dst, load_sem.at[i])
        copy.start()
        loads.append(copy)
    barrier = pltpu.get_barrier_semaphore()
    for d in range(1, n_grid):
        pl.semaphore_signal(barrier, inc=1, device_id={"grid": lax.rem(me + d, n_grid)}, device_id_type=MESH)
    for d in range(1, n_con):
        pl.semaphore_signal(barrier, inc=1, device_id={"con": lax.rem(zc + d, n_con)}, device_id_type=MESH)

    def a2a_copy(peer):
        return pltpu.make_async_remote_copy(
            src_ref=send.at[peer], dst_ref=recv.at[me],
            send_sem=a2a_send.at[peer], recv_sem=a2a_recv.at[me],
            device_id={"grid": peer}, device_id_type=MESH)

    def a2a_arrival(peer):
        return pltpu.make_async_remote_copy(
            src_ref=send.at[peer], dst_ref=recv.at[peer],
            send_sem=a2a_send.at[peer], recv_sem=a2a_recv.at[peer],
            device_id={"grid": peer}, device_id_type=MESH)

    def peer_in(step, slot):
        block = partner(own, step, n_blk)
        return block * pack + slot

    loads[0].wait()
    loads[1].wait()

    def solve_x(step):
        block = partner(own, step, n_blk)
        field = seed[:, :, :, lanes(block)].reshape(n_cp * rows, BLK)
        turned = lax.dot_general(ix[block], field, LAST, preferred_element_type=F32).astype(BF16)
        for half in range(pack):
            send[block * pack + half] = turned[half * rows:(half + 1) * rows]

    steps(1, n_blk, solve_x)
    solve_x(0)
    recv[me] = send[me]

    loads[2].wait()

    def square(block):
        cols = lanes(block)
        total = jnp.zeros((rows, BLK), F32)
        for c in range(con_local):
            v0 = vel[c, 0, :, cols].astype(F32)
            v1 = vel[c, 1, :, cols].astype(F32)
            total = total + w_ref[c] * (v0 * v0 + v1 * v1)
        sq_part[:, cols] = total
        sq_send[:, cols] = total.astype(BF16)

    steps(0, n_blk, square)

    pl.semaphore_wait(barrier, n_grid - 1 + n_con - 1)
    for slot in range(1, pack):
        a2a_copy(own * pack + lax.rem(core + slot, pack)).start()

    def send_step(step):
        for slot in range(pack):
            a2a_copy(peer_in(step, slot)).start()

    steps(1, n_blk, send_step)

    def share_of(index):
        return pl.ds(pl.multiple_of(index * share, share), share)

    def sq_scatter(d):
        peer = lax.rem(zc + d, n_con)
        return pltpu.make_async_remote_copy(
            src_ref=sq_send.at[share_of(peer)], dst_ref=sq_rs.at[d - 1],
            send_sem=sq_send_sem.at[0, d - 1], recv_sem=sq_recv_sem.at[0, d - 1],
            device_id={"con": peer}, device_id_type=MESH)

    def sq_gather(d):
        peer = lax.rem(zc + d, n_con)
        return pltpu.make_async_remote_copy(
            src_ref=sq_ag.at[share_of(zc)], dst_ref=sq_ag.at[share_of(zc)],
            send_sem=sq_send_sem.at[1, d - 1], recv_sem=sq_recv_sem.at[1, d - 1],
            device_id={"con": peer}, device_id_type=MESH)

    def sq_gathered(d):
        source = lax.rem(zc + n_con - d, n_con)
        return pltpu.make_async_remote_copy(
            src_ref=sq_ag.at[share_of(zc)], dst_ref=sq_ag.at[share_of(source)],
            send_sem=sq_send_sem.at[1, d - 1], recv_sem=sq_recv_sem.at[1, d - 1],
            device_id={"con": source}, device_id_type=MESH)

    for d in range(1, n_con):
        sq_scatter(d).start()

    loads[3].wait()
    loads[4].wait()
    lane = lax.broadcasted_iota(jnp.int32, (BLK, BLK), 1)
    lane_m = lax.broadcasted_iota(jnp.int32, (rows, BLK), 1)

    def spread(tile, lane_of, place, source):
        shift = (place - source) * rows % BLK
        moved = pltpu.roll(tile, shift, 1) if shift else tile
        return jnp.where(lax.div(lane_of, rows) == place, moved, 0.0)

    def prepare(block):
        tile = iy[block].astype(F32)
        sea = (land[:, lanes(block)] == 1).astype(F32)
        for source in range(pack):
            spot = slice(source * BLK, (source + 1) * BLK)
            if pack == 1:
                wide[block] = iy[block]
                mask[block] = sea.astype(BF16)
            else:
                both = jnp.zeros((rows, BLK), F32)
                for place in range(pack):
                    wide[block, place * BLK:(place + 1) * BLK, spot] = spread(tile, lane, place, source).astype(BF16)
                    both = both + spread(sea, lane_m, place, source)
                mask[block, :, spot] = both.astype(BF16)

    steps(0, n_blk, prepare)

    for d in range(1, n_con):
        sq_scatter(d).wait_recv()
    total = sq_part[share_of(zc)]
    for d in range(1, n_con):
        total = total + sq_rs[d - 1].astype(F32)
    sq_ag[share_of(zc)] = total.astype(BF16)
    for d in range(1, n_con):
        sq_gather(d).start()

    def in_scatter(step, d):
        peer = lax.rem(zc + d, n_con)
        return pltpu.make_async_remote_copy(
            src_ref=in_send.at[step, share_of(peer)], dst_ref=in_rs.at[step, d - 1],
            send_sem=in_send_sem.at[0, step, d - 1], recv_sem=in_recv_sem.at[0, step, d - 1],
            device_id={"con": peer}, device_id_type=MESH)

    def in_gather(step, d):
        peer = lax.rem(zc + d, n_con)
        return pltpu.make_async_remote_copy(
            src_ref=in_ag.at[step, share_of(zc)], dst_ref=in_ag.at[step, share_of(zc)],
            send_sem=in_send_sem.at[1, step, d - 1], recv_sem=in_recv_sem.at[1, step, d - 1],
            device_id={"con": peer}, device_id_type=MESH)

    def in_gathered(step, d):
        source = lax.rem(zc + n_con - d, n_con)
        return pltpu.make_async_remote_copy(
            src_ref=in_ag.at[step, share_of(zc)], dst_ref=in_ag.at[step, share_of(source)],
            send_sem=in_send_sem.at[1, step, d - 1], recv_sem=in_recv_sem.at[1, step, d - 1],
            device_id={"con": source}, device_id_type=MESH)

    def solve_y(step, waits):
        for peer in waits:
            a2a_arrival(peer).wait_recv()
        block = partner(own, step, n_blk)
        cols = lanes(block)
        weight = wide[block]
        keep = mask[block]
        parts = []
        for q in range(groups):
            pieces = [recv[block * pack + source, :, q * BLK:(q + 1) * BLK] for source in range(pack)]
            parts.append((pieces[0] if pack == 1 else jnp.concatenate(pieces, axis=1)) * keep)
        solved = lax.dot_general(jnp.concatenate(parts, axis=0), weight, LAST, preferred_element_type=F32)
        total = jnp.zeros((rows, BLK), F32)
        for cp in range(n_cp):
            q, place = cp // pack, cp % pack
            value = solved[q * rows:(q + 1) * rows, place * BLK:(place + 1) * BLK]
            rhs[cp, :, cols] = value
            total = total + value * vel[cp // 2, cp % 2, :, cols].astype(F32)
        in_part[step] = total
        in_send[step] = total.astype(BF16)
        for d in range(1, n_con):
            in_scatter(step, d).start()

    def reduce_inner(step):
        for d in range(1, n_con):
            in_scatter(step, d).wait_recv()
        mine = in_part[step, share_of(zc)]
        for d in range(1, n_con):
            mine = mine + in_rs[step, d - 1].astype(F32)
        in_ag[step, share_of(zc)] = mine.astype(BF16)
        for d in range(1, n_con):
            in_gather(step, d).start()

    solve_y(0, [own * pack + lax.rem(core + slot, pack) for slot in range(1, pack)])

    def step_y(step):
        solve_y(step, [peer_in(step, slot) for slot in range(pack)])
        reduce_inner(step - 1)

    steps(1, n_blk, step_y)
    reduce_inner(n_blk - 1)

    for d in range(1, n_con):
        sq_gathered(d).wait_recv()

    def factors(block):
        cols = lanes(block)
        squared = 0.25 + sq_ag[:, cols].astype(F32)
        inverse = lax.rsqrt(squared)
        half = jnp.where(land[:, cols] == 1, -0.5, 0.0)
        ca[:, cols] = half * (squared * inverse)
        cb[:, cols] = half * inverse

    steps(0, n_blk, factors)

    def finish(step):
        for d in range(1, n_con):
            in_gathered(step, d).wait_recv()
        cols = lanes(partner(own, step, n_blk))
        first = ca[:, cols]
        second = cb[:, cols] * in_ag[step].astype(F32)
        for c in range(con_local):
            scaled = w_ref[c] * second
            for p in range(2):
                out_ref[c, p, :, cols] = first * rhs[2 * c + p, :, cols] + scaled * vel[c, p, :, cols].astype(F32)

    steps(0, n_blk, finish)

    for slot in range(1, pack):
        a2a_copy(own * pack + lax.rem(core + slot, pack)).wait_send()

    def left(step):
        for slot in range(pack):
            a2a_copy(peer_in(step, slot)).wait_send()

    steps(1, n_blk, left)
    for d in range(1, n_con):
        sq_scatter(d).wait_send()
        sq_gather(d).wait_send()

    def in_left(step):
        for d in range(1, n_con):
            in_scatter(step, d).wait_send()
            in_gather(step, d).wait_send()

    steps(0, n_blk, in_left)


def local(n_con, n_grid, velocity, seed_adjoint, land_mask, inv_x, inv_y, weights):
    con_local, _, rows, side = velocity.shape
    n_blk = inv_x.shape[0]
    pack = BLK // rows
    n_cp = 2 * con_local
    dims = (n_con, n_grid, n_blk, con_local, rows, side)
    share = rows // n_con
    vm = pltpu.VMEM
    sem = pltpu.SemaphoreType.DMA
    peers = max(n_con - 1, 1)
    scratch = [
        vm(velocity.shape, BF16), vm(seed_adjoint.shape, BF16), vm(land_mask.shape, jnp.int32),
        vm(inv_x.shape, BF16), vm(inv_y.shape, BF16),
        vm((n_grid, rows, n_cp * rows), BF16), vm((n_grid, rows, n_cp * rows), BF16),
        vm((n_blk, pack * BLK, pack * BLK), BF16), vm((n_blk, rows, pack * BLK), BF16),
        vm((rows, side), F32), vm((rows, side), BF16), vm((peers, share, side), BF16), vm((rows, side), BF16),
        vm((n_cp, rows, side), F32), vm((n_blk, rows, BLK), F32), vm((n_blk, rows, BLK), BF16),
        vm((n_blk, peers, share, BLK), BF16), vm((n_blk, rows, BLK), BF16),
        vm((rows, side), F32), vm((rows, side), F32),
        sem((5,)), sem((n_grid,)), sem((n_grid,)),
        sem((2, peers)), sem((2, peers)), sem((2, n_blk, peers)), sem((2, n_blk, peers)),
    ]
    anywhere = pl.BlockSpec(memory_space=pl.ANY)
    flops = 2 * 2 * n_cp * rows * side * BLK
    return pl.pallas_call(
        functools.partial(kernel, dims),
        out_shape=jax.ShapeDtypeStruct(velocity.shape, F32),
        in_specs=[anywhere] * 5 + [pl.BlockSpec(memory_space=pltpu.SMEM)],
        out_specs=pl.BlockSpec(memory_space=pltpu.VMEM),
        scratch_shapes=scratch,
        cost_estimate=pl.CostEstimate(flops=flops, bytes_accessed=4 * velocity.size * 2, transcendentals=rows * side),
        compiler_params=pltpu.CompilerParams(
            collective_id=0, has_side_effects=True, vmem_limit_bytes=58 * 1024 * 1024),
    )(velocity, seed_adjoint, land_mask, inv_x, inv_y, weights)


def solution(mesh):
    return jax.shard_map(
        functools.partial(local, mesh.shape["con"], mesh.shape["grid"]),
        mesh=mesh,
        in_specs=(
            P("con", None, "grid", None),
            P("con", None, "grid", None),
            P("grid", None),
            P(),
            P(),
            P("con"),
        ),
        out_specs=P("con", None, "grid", None),
        check_vma=False,
    )
```

```python
import functools
import math
import jax
import jax.numpy as jnp
from jax import lax
from jax.experimental import pallas as pl
from jax.experimental.pallas import tpu as pltpu
from jax.sharding import PartitionSpec as P

BLK = 128
MESH = pl.DeviceIdType.MESH
F32, BF16 = jnp.float32, jnp.bfloat16
LAST = (((1,), (1,)), ((), ()))


def partner(own, step, count):
    if count & (count - 1):
        return lax.rem(own + step, count)
    total, bit = 0, 1
    while bit < count:
        mine = lax.rem(lax.div(own, bit), 2)
        turn = step // bit % 2 if isinstance(step, int) else lax.rem(lax.div(step, bit), 2)
        total = total + lax.rem(mine + turn, 2) * bit
        bit *= 2
    return total


def steps(first, stop, body):
    if stop - first <= 8:
        for step in range(first, stop):
            body(step)
    else:
        @pl.loop(first, stop)
        def _(step):
            body(step)


def lanes(block):
    return pl.ds(pl.multiple_of(block * BLK, BLK), BLK)


def kernel(
    dims,
    vel_hbm, seed_hbm, land_hbm, ix_hbm, iy_hbm, w_hbm,
    out_ref,
    vel, seed, land, ix, iy, w_ref,
    send, recv, wide, mask,
    sq_part, sq_send, sq_rs, sq_ag,
    rhs, in_part, in_send, in_rs, in_ag, ca, cb,
    load_sem, a2a_send, a2a_recv, sq_send_sem, sq_recv_sem, in_send_sem, in_recv_sem,
):
    n_con, n_grid, n_blk, con_local, rows, side = dims
    pack = BLK // rows
    n_cp = con_local * 2
    groups = n_cp // pack
    share = rows // n_con
    me = lax.axis_index("grid")
    zc = lax.axis_index("con")
    own = lax.div(me, pack)
    core = lax.rem(me, pack)

    barrier = pltpu.get_barrier_semaphore()
    for d in range(1, n_grid):
        pl.semaphore_signal(barrier, inc=1, device_id={"grid": lax.rem(me + d, n_grid)}, device_id_type=MESH)
    for d in range(1, n_con):
        pl.semaphore_signal(barrier, inc=1, device_id={"con": lax.rem(zc + d, n_con)}, device_id_type=MESH)

    loads = []
    for i, (src, dst) in enumerate(((seed_hbm, seed), (ix_hbm, ix), (vel_hbm, vel), (w_hbm, w_ref), (iy_hbm, iy), (land_hbm, land))):
        copy = pltpu.make_async_copy(src, dst, load_sem.at[i])
        copy.start()
        loads.append(copy)

    def a2a_copy(peer):
        return pltpu.make_async_remote_copy(
            src_ref=send.at[peer], dst_ref=recv.at[me],
            send_sem=a2a_send.at[peer], recv_sem=a2a_recv.at[me],
            device_id={"grid": peer}, device_id_type=MESH)

    def a2a_arrival(peer):
        return pltpu.make_async_remote_copy(
            src_ref=send.at[peer], dst_ref=recv.at[peer],
            send_sem=a2a_send.at[peer], recv_sem=a2a_recv.at[peer],
            device_id={"grid": peer}, device_id_type=MESH)

    def peer_in(step, slot):
        block = partner(own, step, n_blk)
        return block * pack + slot

    loads[0].wait()
    loads[1].wait()

    def solve_x(step):
        block = partner(own, step, n_blk)
        field = seed[:, :, :, lanes(block)].reshape(n_cp * rows, BLK)
        turned = lax.dot_general(ix[block], field, LAST, preferred_element_type=F32).astype(BF16)
        for half in range(pack):
            send[block * pack + half] = turned[half * rows:(half + 1) * rows]

    pl.semaphore_wait(barrier, n_grid - 1 + n_con - 1)

    def solve_and_send(step):
        solve_x(step)
        for slot in range(pack):
            a2a_copy(peer_in(step, slot)).start()

    steps(1, n_blk, solve_and_send)
    solve_x(0)
    for slot in range(1, pack):
        a2a_copy(own * pack + lax.rem(core + slot, pack)).start()
    recv[me] = send[me]

    loads[2].wait()
    loads[3].wait()

    def square(block):
        cols = lanes(block)
        total = jnp.zeros((rows, BLK), F32)
        for c in range(con_local):
            v0 = vel[c, 0, :, cols].astype(F32)
            v1 = vel[c, 1, :, cols].astype(F32)
            total = total + w_ref[c] * (v0 * v0 + v1 * v1)
        sq_part[:, cols] = total
        sq_send[:, cols] = total.astype(BF16)

    steps(0, n_blk, square)

    def share_of(index):
        return pl.ds(pl.multiple_of(index * share, share), share)

    def sq_scatter(d):
        peer = lax.rem(zc + d, n_con)
        return pltpu.make_async_remote_copy(
            src_ref=sq_send.at[share_of(peer)], dst_ref=sq_rs.at[d - 1],
            send_sem=sq_send_sem.at[0, d - 1], recv_sem=sq_recv_sem.at[0, d - 1],
            device_id={"con": peer}, device_id_type=MESH)

    def sq_gather(d):
        peer = lax.rem(zc + d, n_con)
        return pltpu.make_async_remote_copy(
            src_ref=sq_ag.at[share_of(zc)], dst_ref=sq_ag.at[share_of(zc)],
            send_sem=sq_send_sem.at[1, d - 1], recv_sem=sq_recv_sem.at[1, d - 1],
            device_id={"con": peer}, device_id_type=MESH)

    def sq_gathered(d):
        source = lax.rem(zc + n_con - d, n_con)
        return pltpu.make_async_remote_copy(
            src_ref=sq_ag.at[share_of(zc)], dst_ref=sq_ag.at[share_of(source)],
            send_sem=sq_send_sem.at[1, d - 1], recv_sem=sq_recv_sem.at[1, d - 1],
            device_id={"con": source}, device_id_type=MESH)

    for d in range(1, n_con):
        sq_scatter(d).start()

    loads[4].wait()
    loads[5].wait()
    lane = lax.broadcasted_iota(jnp.int32, (BLK, BLK), 1)
    lane_m = lax.broadcasted_iota(jnp.int32, (rows, BLK), 1)

    def spread(tile, lane_of, place, source):
        shift = (place - source) * rows % BLK
        moved = pltpu.roll(tile, shift, 1) if shift else tile
        return jnp.where(lax.div(lane_of, rows) == place, moved, 0.0)

    def prepare(block):
        tile = iy[block].astype(F32)
        sea = (land[:, lanes(block)] == 1).astype(F32)
        for source in range(pack):
            spot = slice(source * BLK, (source + 1) * BLK)
            if pack == 1:
                wide[block] = iy[block]
                mask[block] = sea.astype(BF16)
            else:
                both = jnp.zeros((rows, BLK), F32)
                for place in range(pack):
                    wide[block, place * BLK:(place + 1) * BLK, spot] = spread(tile, lane, place, source).astype(BF16)
                    both = both + spread(sea, lane_m, place, source)
                mask[block, :, spot] = both.astype(BF16)

    steps(0, n_blk, prepare)

    for d in range(1, n_con):
        sq_scatter(d).wait_recv()
    total = sq_part[share_of(zc)]
    for d in range(1, n_con):
        total = total + sq_rs[d - 1].astype(F32)
    sq_ag[share_of(zc)] = total.astype(BF16)
    for d in range(1, n_con):
        sq_gather(d).start()

    def in_scatter(step, d):
        peer = lax.rem(zc + d, n_con)
        return pltpu.make_async_remote_copy(
            src_ref=in_send.at[step, share_of(peer)], dst_ref=in_rs.at[step, d - 1],
            send_sem=in_send_sem.at[0, step, d - 1], recv_sem=in_recv_sem.at[0, step, d - 1],
            device_id={"con": peer}, device_id_type=MESH)

    def in_gather(step, d):
        peer = lax.rem(zc + d, n_con)
        return pltpu.make_async_remote_copy(
            src_ref=in_ag.at[step, share_of(zc)], dst_ref=in_ag.at[step, share_of(zc)],
            send_sem=in_send_sem.at[1, step, d - 1], recv_sem=in_recv_sem.at[1, step, d - 1],
            device_id={"con": peer}, device_id_type=MESH)

    def in_gathered(step, d):
        source = lax.rem(zc + n_con - d, n_con)
        return pltpu.make_async_remote_copy(
            src_ref=in_ag.at[step, share_of(zc)], dst_ref=in_ag.at[step, share_of(source)],
            send_sem=in_send_sem.at[1, step, d - 1], recv_sem=in_recv_sem.at[1, step, d - 1],
            device_id={"con": source}, device_id_type=MESH)

    def solve_y(step, waits):
        for peer in waits:
            a2a_arrival(peer).wait_recv()
        block = partner(own, step, n_blk)
        cols = lanes(block)
        weight = wide[block]
        keep = mask[block]
        parts = []
        for q in range(groups):
            pieces = [recv[block * pack + source, :, q * BLK:(q + 1) * BLK] for source in range(pack)]
            parts.append((pieces[0] if pack == 1 else jnp.concatenate(pieces, axis=1)) * keep)
        solved = lax.dot_general(jnp.concatenate(parts, axis=0), weight, LAST, preferred_element_type=F32)
        total = jnp.zeros((rows, BLK), F32)
        for cp in range(n_cp):
            q, place = cp // pack, cp % pack
            value = solved[q * rows:(q + 1) * rows, place * BLK:(place + 1) * BLK]
            rhs[cp, :, cols] = value
            total = total + value * vel[cp // 2, cp % 2, :, cols].astype(F32)
        in_part[step] = total
        in_send[step] = total.astype(BF16)
        for d in range(1, n_con):
            in_scatter(step, d).start()

    def reduce_inner(step):
        for d in range(1, n_con):
            in_scatter(step, d).wait_recv()
        mine = in_part[step, share_of(zc)]
        for d in range(1, n_con):
            mine = mine + in_rs[step, d - 1].astype(F32)
        in_ag[step, share_of(zc)] = mine.astype(BF16)
        for d in range(1, n_con):
            in_gather(step, d).start()

    solve_y(0, [own * pack + lax.rem(core + slot, pack) for slot in range(1, pack)])

    def step_y(step):
        solve_y(step, [peer_in(step, slot) for slot in range(pack)])
        reduce_inner(step - 1)

    steps(1, n_blk, step_y)
    reduce_inner(n_blk - 1)

    for d in range(1, n_con):
        sq_gathered(d).wait_recv()

    def factors(block):
        cols = lanes(block)
        squared = 0.25 + sq_ag[:, cols].astype(F32)
        inverse = lax.rsqrt(squared)
        half = jnp.where(land[:, cols] == 1, -0.5, 0.0)
        ca[:, cols] = half * (squared * inverse)
        cb[:, cols] = half * inverse

    steps(0, n_blk, factors)

    def finish(step):
        for d in range(1, n_con):
            in_gathered(step, d).wait_recv()
        cols = lanes(partner(own, step, n_blk))
        first = ca[:, cols]
        second = cb[:, cols] * in_ag[step].astype(F32)
        for c in range(con_local):
            scaled = w_ref[c] * second
            for p in range(2):
                out_ref[c, p, :, cols] = first * rhs[2 * c + p, :, cols] + scaled * vel[c, p, :, cols].astype(F32)

    steps(0, n_blk, finish)

    for slot in range(1, pack):
        a2a_copy(own * pack + lax.rem(core + slot, pack)).wait_send()

    def left(step):
        for slot in range(pack):
            a2a_copy(peer_in(step, slot)).wait_send()

    steps(1, n_blk, left)
    for d in range(1, n_con):
        sq_scatter(d).wait_send()
        sq_gather(d).wait_send()

    def in_left(step):
        for d in range(1, n_con):
            in_scatter(step, d).wait_send()
            in_gather(step, d).wait_send()

    steps(0, n_blk, in_left)


def local(n_con, n_grid, velocity, seed_adjoint, land_mask, inv_x, inv_y, weights):
    con_local, _, rows, side = velocity.shape
    n_blk = inv_x.shape[0]
    pack = BLK // rows
    n_cp = 2 * con_local
    dims = (n_con, n_grid, n_blk, con_local, rows, side)
    share = rows // n_con
    vm = pltpu.VMEM
    sem = pltpu.SemaphoreType.DMA
    peers = max(n_con - 1, 1)
    scratch = [
        vm(velocity.shape, BF16), vm(seed_adjoint.shape, BF16), vm(land_mask.shape, jnp.int32),
        vm(inv_x.shape, BF16), vm(inv_y.shape, BF16), pltpu.SMEM(weights.shape, F32),
        vm((n_grid, rows, n_cp * rows), BF16), vm((n_grid, rows, n_cp * rows), BF16),
        vm((n_blk, pack * BLK, pack * BLK), BF16), vm((n_blk, rows, pack * BLK), BF16),
        vm((rows, side), F32), vm((rows, side), BF16), vm((peers, share, side), BF16), vm((rows, side), BF16),
        vm((n_cp, rows, side), F32), vm((n_blk, rows, BLK), F32), vm((n_blk, rows, BLK), BF16),
        vm((n_blk, peers, share, BLK), BF16), vm((n_blk, rows, BLK), BF16),
        vm((rows, side), F32), vm((rows, side), F32),
        sem((6,)), sem((n_grid,)), sem((n_grid,)),
        sem((2, peers)), sem((2, peers)), sem((2, n_blk, peers)), sem((2, n_blk, peers)),
    ]
    held = sum(math.prod(spec.shape) * jnp.dtype(spec.dtype).itemsize for spec in scratch[:21])
    limit = held + velocity.size * 4 + max(4 << 20, velocity.size * 4)
    anywhere = pl.BlockSpec(memory_space=pltpu.HBM)
    flops = 2 * 2 * n_cp * rows * side * BLK
    return pl.pallas_call(
        functools.partial(kernel, dims),
        out_shape=jax.ShapeDtypeStruct(velocity.shape, F32),
        in_specs=[anywhere] * 6,
        out_specs=pl.BlockSpec(memory_space=pltpu.VMEM),
        scratch_shapes=scratch,
        cost_estimate=pl.CostEstimate(flops=flops, bytes_accessed=4 * velocity.size * 2, transcendentals=rows * side),
        compiler_params=pltpu.CompilerParams(
            collective_id=0, has_side_effects=True, vmem_limit_bytes=limit),
    )(velocity, seed_adjoint, land_mask, inv_x, inv_y, weights)


def solution(mesh):
    return jax.shard_map(
        functools.partial(local, mesh.shape["con"], mesh.shape["grid"]),
        mesh=mesh,
        in_specs=(
            P("con", None, "grid", None),
            P("con", None, "grid", None),
            P("grid", None),
            P(),
            P(),
            P("con"),
        ),
        out_specs=P("con", None, "grid", None),
        check_vma=False,
    )
```

```python
import functools
import math
import jax
import jax.numpy as jnp
from jax import lax
from jax.experimental import pallas as pl
from jax.experimental.pallas import tpu as pltpu
from jax.sharding import PartitionSpec as P

BLK = 128
MESH = pl.DeviceIdType.MESH
F32, BF16 = jnp.float32, jnp.bfloat16
LAST = (((1,), (1,)), ((), ()))


def partner(own, step, count):
    if count & (count - 1):
        return lax.rem(own + step, count)
    total, bit = 0, 1
    while bit < count:
        mine = lax.rem(lax.div(own, bit), 2)
        turn = step // bit % 2 if isinstance(step, int) else lax.rem(lax.div(step, bit), 2)
        total = total + lax.rem(mine + turn, 2) * bit
        bit *= 2
    return total


def steps(first, stop, body):
    if stop - first <= 8:
        for step in range(first, stop):
            body(step)
    else:
        @pl.loop(first, stop)
        def _(step):
            body(step)


def lanes(block):
    return pl.ds(pl.multiple_of(block * BLK, BLK), BLK)


def kernel(
    dims,
    vel_hbm, seed_hbm, land_hbm, ix_hbm, iy_hbm, w_hbm,
    out_ref,
    vel, seed, land, ix, iy, w_ref,
    send, recv, wide, mask,
    sq_part, sq_send, sq_rs, sq_ag,
    rhs, in_part, in_send, in_rs, in_ag, ca, cb,
    load_sem, a2a_send, a2a_recv, sq_send_sem, sq_recv_sem, in_send_sem, in_recv_sem,
):
    n_con, n_grid, n_blk, con_local, rows, side = dims
    pack = BLK // rows
    n_cp = con_local * 2
    groups = n_cp // pack
    share = rows // n_con
    me = lax.axis_index("grid")
    zc = lax.axis_index("con")
    own = lax.div(me, pack)
    core = lax.rem(me, pack)

    barrier = pltpu.get_barrier_semaphore()
    for d in range(1, n_grid):
        pl.semaphore_signal(barrier, inc=1, device_id={"grid": lax.rem(me + d, n_grid)}, device_id_type=MESH)
    for d in range(1, n_con):
        pl.semaphore_signal(barrier, inc=1, device_id={"con": lax.rem(zc + d, n_con)}, device_id_type=MESH)

    loads = []
    for i, (src, dst) in enumerate(((seed_hbm, seed), (ix_hbm, ix), (vel_hbm, vel), (w_hbm, w_ref), (iy_hbm, iy), (land_hbm, land))):
        copy = pltpu.make_async_copy(src, dst, load_sem.at[i])
        copy.start()
        loads.append(copy)

    def a2a_copy(peer):
        return pltpu.make_async_remote_copy(
            src_ref=send.at[peer], dst_ref=recv.at[me],
            send_sem=a2a_send.at[peer], recv_sem=a2a_recv.at[me],
            device_id={"grid": peer}, device_id_type=MESH)

    def a2a_arrival(peer):
        return pltpu.make_async_remote_copy(
            src_ref=send.at[peer], dst_ref=recv.at[peer],
            send_sem=a2a_send.at[peer], recv_sem=a2a_recv.at[peer],
            device_id={"grid": peer}, device_id_type=MESH)

    def peer_in(step, slot):
        block = partner(own, step, n_blk)
        return block * pack + slot

    loads[0].wait()
    loads[1].wait()

    def solve_x(step):
        block = partner(own, step, n_blk)
        field = seed[:, :, :, lanes(block)].reshape(n_cp * rows, BLK)
        turned = lax.dot_general(ix[block], field, LAST, preferred_element_type=F32).astype(BF16)
        for half in range(pack):
            send[block * pack + half] = turned[half * rows:(half + 1) * rows]

    pl.semaphore_wait(barrier, n_grid - 1 + n_con - 1)

    def solve_and_send(step):
        solve_x(step)
        for slot in range(pack):
            a2a_copy(peer_in(step, slot)).start()

    steps(1, n_blk, solve_and_send)
    solve_x(0)
    for slot in range(1, pack):
        a2a_copy(own * pack + lax.rem(core + slot, pack)).start()
    recv[me] = send[me]

    loads[2].wait()
    loads[3].wait()

    def square(block):
        cols = lanes(block)
        total = jnp.zeros((rows, BLK), F32)
        for c in range(con_local):
            v0 = vel[c, 0, :, cols].astype(F32)
            v1 = vel[c, 1, :, cols].astype(F32)
            total = total + w_ref[c] * (v0 * v0 + v1 * v1)
        sq_part[:, cols] = total
        sq_send[:, cols] = total.astype(BF16)

    steps(0, n_blk, square)

    def share_of(index):
        return pl.ds(pl.multiple_of(index * share, share), share)

    def sq_scatter(d):
        peer = lax.rem(zc + d, n_con)
        return pltpu.make_async_remote_copy(
            src_ref=sq_send.at[share_of(peer)], dst_ref=sq_rs.at[d - 1],
            send_sem=sq_send_sem.at[0, d - 1], recv_sem=sq_recv_sem.at[0, d - 1],
            device_id={"con": peer}, device_id_type=MESH)

    def sq_gather(d):
        peer = lax.rem(zc + d, n_con)
        return pltpu.make_async_remote_copy(
            src_ref=sq_ag.at[share_of(zc)], dst_ref=sq_ag.at[share_of(zc)],
            send_sem=sq_send_sem.at[1, d - 1], recv_sem=sq_recv_sem.at[1, d - 1],
            device_id={"con": peer}, device_id_type=MESH)

    def sq_gathered(d):
        source = lax.rem(zc + n_con - d, n_con)
        return pltpu.make_async_remote_copy(
            src_ref=sq_ag.at[share_of(zc)], dst_ref=sq_ag.at[share_of(source)],
            send_sem=sq_send_sem.at[1, d - 1], recv_sem=sq_recv_sem.at[1, d - 1],
            device_id={"con": source}, device_id_type=MESH)

    for d in range(1, n_con):
        sq_scatter(d).start()

    loads[4].wait()
    loads[5].wait()
    lane = lax.broadcasted_iota(jnp.int32, (BLK, BLK), 1)
    lane_m = lax.broadcasted_iota(jnp.int32, (rows, BLK), 1)

    def spread(tile, lane_of, place, source):
        shift = (place - source) * rows % BLK
        moved = pltpu.roll(tile, shift, 1) if shift else tile
        return jnp.where(lax.div(lane_of, rows) == place, moved, 0.0)

    def prepare(block):
        tile = iy[block].astype(F32)
        sea = (land[:, lanes(block)] == 1).astype(F32)
        for source in range(pack):
            spot = slice(source * BLK, (source + 1) * BLK)
            if pack == 1:
                wide[block] = iy[block]
                mask[block] = sea.astype(BF16)
            else:
                both = jnp.zeros((rows, BLK), F32)
                for place in range(pack):
                    wide[block, place * BLK:(place + 1) * BLK, spot] = spread(tile, lane, place, source).astype(BF16)
                    both = both + spread(sea, lane_m, place, source)
                mask[block, :, spot] = both.astype(BF16)

    steps(0, n_blk, prepare)

    for d in range(1, n_con):
        sq_scatter(d).wait_recv()
    total = sq_part[share_of(zc)]
    for d in range(1, n_con):
        total = total + sq_rs[d - 1].astype(F32)
    sq_ag[share_of(zc)] = total.astype(BF16)
    for d in range(1, n_con):
        sq_gather(d).start()

    def in_scatter(step, d):
        peer = lax.rem(zc + d, n_con)
        return pltpu.make_async_remote_copy(
            src_ref=in_send.at[step, share_of(peer)], dst_ref=in_rs.at[step, d - 1],
            send_sem=in_send_sem.at[0, step, d - 1], recv_sem=in_recv_sem.at[0, step, d - 1],
            device_id={"con": peer}, device_id_type=MESH)

    def in_gather(step, d):
        peer = lax.rem(zc + d, n_con)
        return pltpu.make_async_remote_copy(
            src_ref=in_ag.at[step, share_of(zc)], dst_ref=in_ag.at[step, share_of(zc)],
            send_sem=in_send_sem.at[1, step, d - 1], recv_sem=in_recv_sem.at[1, step, d - 1],
            device_id={"con": peer}, device_id_type=MESH)

    def in_gathered(step, d):
        source = lax.rem(zc + n_con - d, n_con)
        return pltpu.make_async_remote_copy(
            src_ref=in_ag.at[step, share_of(zc)], dst_ref=in_ag.at[step, share_of(source)],
            send_sem=in_send_sem.at[1, step, d - 1], recv_sem=in_recv_sem.at[1, step, d - 1],
            device_id={"con": source}, device_id_type=MESH)

    def solve_y(step, waits):
        for peer in waits:
            a2a_arrival(peer).wait_recv()
        block = partner(own, step, n_blk)
        cols = lanes(block)
        weight = wide[block]
        keep = mask[block]
        parts = []
        for q in range(groups):
            pieces = [recv[block * pack + source, :, q * BLK:(q + 1) * BLK] for source in range(pack)]
            parts.append((pieces[0] if pack == 1 else jnp.concatenate(pieces, axis=1)) * keep)
        solved = lax.dot_general(jnp.concatenate(parts, axis=0), weight, LAST, preferred_element_type=F32)
        total = jnp.zeros((rows, BLK), F32)
        for cp in range(n_cp):
            q, place = cp // pack, cp % pack
            value = solved[q * rows:(q + 1) * rows, place * BLK:(place + 1) * BLK]
            rhs[cp, :, cols] = value
            total = total + value * vel[cp // 2, cp % 2, :, cols].astype(F32)
        in_part[step] = total
        in_send[step] = total.astype(BF16)
        for d in range(1, n_con):
            in_scatter(step, d).start()

    def reduce_inner(step):
        for d in range(1, n_con):
            in_scatter(step, d).wait_recv()
        mine = in_part[step, share_of(zc)]
        for d in range(1, n_con):
            mine = mine + in_rs[step, d - 1].astype(F32)
        in_ag[step, share_of(zc)] = mine.astype(BF16)
        for d in range(1, n_con):
            in_gather(step, d).start()

    solve_y(0, [own * pack + lax.rem(core + slot, pack) for slot in range(1, pack)])

    def step_y(step):
        solve_y(step, [peer_in(step, slot) for slot in range(pack)])
        reduce_inner(step - 1)

    steps(1, n_blk, step_y)
    reduce_inner(n_blk - 1)

    for d in range(1, n_con):
        sq_gathered(d).wait_recv()

    def factors(block):
        cols = lanes(block)
        squared = 0.25 + sq_ag[:, cols].astype(F32)
        inverse = lax.rsqrt(squared)
        half = jnp.where(land[:, cols] == 1, -0.5, 0.0)
        ca[:, cols] = half * (squared * inverse)
        cb[:, cols] = half * inverse

    steps(0, n_blk, factors)

    def finish(step):
        for d in range(1, n_con):
            in_gathered(step, d).wait_recv()
        cols = lanes(partner(own, step, n_blk))
        first = ca[:, cols]
        second = cb[:, cols] * in_ag[step].astype(F32)
        for c in range(con_local):
            scaled = w_ref[c] * second
            for p in range(2):
                out_ref[c, p, :, cols] = first * rhs[2 * c + p, :, cols] + scaled * vel[c, p, :, cols].astype(F32)

    steps(0, n_blk, finish)

    for slot in range(1, pack):
        a2a_copy(own * pack + lax.rem(core + slot, pack)).wait_send()

    def left(step):
        for slot in range(pack):
            a2a_copy(peer_in(step, slot)).wait_send()

    steps(1, n_blk, left)
    for d in range(1, n_con):
        sq_scatter(d).wait_send()
        sq_gather(d).wait_send()

    def in_left(step):
        for d in range(1, n_con):
            in_scatter(step, d).wait_send()
            in_gather(step, d).wait_send()

    steps(0, n_blk, in_left)


def local(n_con, n_grid, velocity, seed_adjoint, land_mask, inv_x, inv_y, weights):
    con_local, _, rows, side = velocity.shape
    n_blk = inv_x.shape[0]
    pack = BLK // rows
    n_cp = 2 * con_local
    dims = (n_con, n_grid, n_blk, con_local, rows, side)
    share = rows // n_con
    vm = pltpu.VMEM
    sem = pltpu.SemaphoreType.DMA
    peers = max(n_con - 1, 1)
    scratch = [
        vm(velocity.shape, BF16), vm(seed_adjoint.shape, BF16), vm(land_mask.shape, jnp.int32),
        vm(inv_x.shape, BF16), vm(inv_y.shape, BF16), pltpu.SMEM(weights.shape, F32),
        vm((n_grid, rows, n_cp * rows), BF16), vm((n_grid, rows, n_cp * rows), BF16),
        vm((n_blk, pack * BLK, pack * BLK), BF16), vm((n_blk, rows, pack * BLK), BF16),
        vm((rows, side), F32), vm((rows, side), BF16), vm((peers, share, side), BF16), vm((rows, side), BF16),
        vm((n_cp, rows, side), F32), vm((n_blk, rows, BLK), F32), vm((n_blk, rows, BLK), BF16),
        vm((n_blk, peers, share, BLK), BF16), vm((n_blk, rows, BLK), BF16),
        vm((rows, side), F32), vm((rows, side), F32),
        sem((6,)), sem((n_grid,)), sem((n_grid,)),
        sem((2, peers)), sem((2, peers)), sem((2, n_blk, peers)), sem((2, n_blk, peers)),
    ]
    held = sum(math.prod(spec.shape) * jnp.dtype(spec.dtype).itemsize for spec in scratch[:21])
    limit = held + velocity.size * 4 + max(4 << 20, velocity.size * 4)
    anywhere = pl.BlockSpec(memory_space=pltpu.HBM)
    flops = 2 * 2 * n_cp * rows * side * BLK
    return pl.pallas_call(
        functools.partial(kernel, dims),
        out_shape=pltpu.VMEM(velocity.shape, F32),
        in_specs=[anywhere] * 6,
        out_specs=pl.BlockSpec(memory_space=pltpu.VMEM),
        scratch_shapes=scratch,
        cost_estimate=pl.CostEstimate(flops=flops, bytes_accessed=4 * velocity.size * 2, transcendentals=rows * side),
        compiler_params=pltpu.CompilerParams(
            collective_id=0, has_side_effects=True, vmem_limit_bytes=limit),
    )(*(pltpu.with_memory_space_constraint(a, pltpu.HBM) for a in (velocity, seed_adjoint, land_mask, inv_x, inv_y, weights)))


def solution(mesh):
    return jax.shard_map(
        functools.partial(local, mesh.shape["con"], mesh.shape["grid"]),
        mesh=mesh,
        in_specs=(
            P("con", None, "grid", None),
            P("con", None, "grid", None),
            P("grid", None),
            P(),
            P(),
            P("con"),
        ),
        out_specs=P("con", None, "grid", None),
        check_vma=False,
    )
```

```python
import functools
import math
import jax
import jax.numpy as jnp
from jax import lax
from jax.experimental import pallas as pl
from jax.experimental.pallas import tpu as pltpu
from jax.sharding import PartitionSpec as P

BLK = 128
MESH = pl.DeviceIdType.MESH
F32, BF16 = jnp.float32, jnp.bfloat16
LAST = (((1,), (1,)), ((), ()))


def partner(own, step, count):
    if count & (count - 1):
        return lax.rem(own + step, count)
    total, bit = 0, 1
    while bit < count:
        mine = lax.rem(lax.div(own, bit), 2)
        turn = step // bit % 2 if isinstance(step, int) else lax.rem(lax.div(step, bit), 2)
        total = total + lax.rem(mine + turn, 2) * bit
        bit *= 2
    return total


def steps(first, stop, body):
    if stop - first <= 8:
        for step in range(first, stop):
            body(step)
    else:
        @pl.loop(first, stop)
        def _(step):
            body(step)


def lanes(block):
    return pl.ds(pl.multiple_of(block * BLK, BLK), BLK)


def kernel(
    dims,
    vel_hbm, seed_hbm, land_hbm, ix_hbm, iy_hbm, w_hbm,
    out_ref,
    vel, seed, land, ix, iy, w_ref,
    send, recv, wide, mask,
    sq_part, sq_send, sq_rs, sq_ag,
    rhs, in_part, in_send, in_rs, in_ag, in_all, ca, cb,
    load_sem, a2a_send, a2a_recv, sq_send_sem, sq_recv_sem, in_send_sem, in_recv_sem,
):
    n_con, n_grid, n_blk, con_local, rows, side = dims
    pack = BLK // rows
    n_cp = con_local * 2
    groups = n_cp // pack
    share = rows // n_con
    me = lax.axis_index("grid")
    zc = lax.axis_index("con")
    own = lax.div(me, pack)
    core = lax.rem(me, pack)

    barrier = pltpu.get_barrier_semaphore()
    for d in range(1, n_grid):
        pl.semaphore_signal(barrier, inc=1, device_id={"grid": lax.rem(me + d, n_grid)}, device_id_type=MESH)
    for d in range(1, n_con):
        pl.semaphore_signal(barrier, inc=1, device_id={"con": lax.rem(zc + d, n_con)}, device_id_type=MESH)

    loads = []
    for i, (src, dst) in enumerate(((seed_hbm, seed), (ix_hbm, ix), (vel_hbm, vel), (w_hbm, w_ref), (iy_hbm, iy), (land_hbm, land))):
        copy = pltpu.make_async_copy(src, dst, load_sem.at[i])
        copy.start()
        loads.append(copy)

    def a2a_copy(peer):
        return pltpu.make_async_remote_copy(
            src_ref=send.at[peer], dst_ref=recv.at[me],
            send_sem=a2a_send.at[0], recv_sem=a2a_recv.at[own],
            device_id={"grid": peer}, device_id_type=MESH)

    def group(ref, send_sem, recv_sem):
        return pltpu.make_async_remote_copy(
            src_ref=ref, dst_ref=ref, send_sem=send_sem, recv_sem=recv_sem,
            device_id={"con": lax.rem(zc + 1, n_con)}, device_id_type=MESH)

    def peer_in(step, slot):
        block = partner(own, step, n_blk)
        return block * pack + slot

    loads[0].wait()
    loads[1].wait()

    def solve_x(step):
        block = partner(own, step, n_blk)
        field = seed[:, :, :, lanes(block)].reshape(n_cp * rows, BLK)
        turned = lax.dot_general(ix[block], field, LAST, preferred_element_type=F32).astype(BF16)
        for half in range(pack):
            send[block * pack + half] = turned[half * rows:(half + 1) * rows]

    pl.semaphore_wait(barrier, n_grid - 1 + n_con - 1)

    def solve_and_send(step):
        solve_x(step)
        for slot in range(pack):
            a2a_copy(peer_in(step, slot)).start()

    steps(1, n_blk, solve_and_send)
    solve_x(0)
    for slot in range(1, pack):
        a2a_copy(own * pack + lax.rem(core + slot, pack)).start()
    recv[me] = send[me]

    loads[2].wait()
    loads[3].wait()

    def square(block):
        cols = lanes(block)
        total = jnp.zeros((rows, BLK), F32)
        for c in range(con_local):
            v0 = vel[c, 0, :, cols].astype(F32)
            v1 = vel[c, 1, :, cols].astype(F32)
            total = total + w_ref[c] * (v0 * v0 + v1 * v1)
        sq_part[:, cols] = total
        sq_send[:, cols] = total.astype(BF16)

    steps(0, n_blk, square)

    def share_of(index):
        return pl.ds(pl.multiple_of(index * share, share), share)

    def sq_scatter(d):
        peer = lax.rem(zc + d, n_con)
        return pltpu.make_async_remote_copy(
            src_ref=sq_send.at[share_of(peer)], dst_ref=sq_rs.at[d - 1],
            send_sem=sq_send_sem.at[0], recv_sem=sq_recv_sem.at[0],
            device_id={"con": peer}, device_id_type=MESH)

    def sq_gather(d):
        peer = lax.rem(zc + d, n_con)
        return pltpu.make_async_remote_copy(
            src_ref=sq_ag.at[share_of(zc)], dst_ref=sq_ag.at[share_of(zc)],
            send_sem=sq_send_sem.at[1], recv_sem=sq_recv_sem.at[1],
            device_id={"con": peer}, device_id_type=MESH)

    for d in range(1, n_con):
        sq_scatter(d).start()

    loads[4].wait()
    loads[5].wait()
    lane = lax.broadcasted_iota(jnp.int32, (BLK, BLK), 1)
    lane_m = lax.broadcasted_iota(jnp.int32, (rows, BLK), 1)

    def spread(tile, lane_of, place, source):
        shift = (place - source) * rows % BLK
        moved = pltpu.roll(tile, shift, 1) if shift else tile
        return jnp.where(lax.div(lane_of, rows) == place, moved, 0.0)

    def prepare(block):
        tile = iy[block].astype(F32)
        sea = (land[:, lanes(block)] == 1).astype(F32)
        for source in range(pack):
            spot = slice(source * BLK, (source + 1) * BLK)
            if pack == 1:
                wide[block] = iy[block]
                mask[block] = sea.astype(BF16)
            else:
                both = jnp.zeros((rows, BLK), F32)
                for place in range(pack):
                    wide[block, place * BLK:(place + 1) * BLK, spot] = spread(tile, lane, place, source).astype(BF16)
                    both = both + spread(sea, lane_m, place, source)
                mask[block, :, spot] = both.astype(BF16)

    steps(0, n_blk, prepare)

    group(sq_rs, sq_send_sem.at[0], sq_recv_sem.at[0]).wait_recv()
    total = sq_part[share_of(zc)]
    for d in range(1, n_con):
        total = total + sq_rs[d - 1].astype(F32)
    sq_ag[share_of(zc)] = total.astype(BF16)
    for d in range(1, n_con):
        sq_gather(d).start()

    middle, last = n_blk // 2, n_blk - 1
    shared = [(j, a, b) for j, (a, b) in enumerate(((0, middle), (middle, last))) if b > a]

    def in_scatter(j, a, b, d):
        peer = lax.rem(zc + d, n_con)
        return pltpu.make_async_remote_copy(
            src_ref=in_send.at[a:b, share_of(peer)], dst_ref=in_rs.at[d - 1, a:b],
            send_sem=in_send_sem.at[0], recv_sem=in_recv_sem.at[0, j],
            device_id={"con": peer}, device_id_type=MESH)

    def in_gather(j, a, b, d):
        peer = lax.rem(zc + d, n_con)
        return pltpu.make_async_remote_copy(
            src_ref=in_ag.at[a:b, share_of(zc)], dst_ref=in_ag.at[a:b, share_of(zc)],
            send_sem=in_send_sem.at[1], recv_sem=in_recv_sem.at[1, j],
            device_id={"con": peer}, device_id_type=MESH)

    def in_straight(d):
        peer = lax.rem(zc + d, n_con)
        return pltpu.make_async_remote_copy(
            src_ref=in_send.at[last], dst_ref=in_all.at[d - 1],
            send_sem=in_send_sem.at[2], recv_sem=in_recv_sem.at[0, 2],
            device_id={"con": peer}, device_id_type=MESH)

    def solve_y(step, arriving=pack):
        block = partner(own, step, n_blk)
        if arriving:
            group(recv.at[pl.ds(block * pack, arriving)], a2a_send.at[0], a2a_recv.at[block]).wait_recv()
        cols = lanes(block)
        weight = wide[block]
        keep = mask[block]
        parts = []
        for q in range(groups):
            pieces = [recv[block * pack + source, :, q * BLK:(q + 1) * BLK] for source in range(pack)]
            parts.append((pieces[0] if pack == 1 else jnp.concatenate(pieces, axis=1)) * keep)
        solved = lax.dot_general(jnp.concatenate(parts, axis=0), weight, LAST, preferred_element_type=F32)
        total = jnp.zeros((rows, BLK), F32)
        for cp in range(n_cp):
            q, place = cp // pack, cp % pack
            value = solved[q * rows:(q + 1) * rows, place * BLK:(place + 1) * BLK]
            rhs[cp, :, cols] = value
            total = total + value * vel[cp // 2, cp % 2, :, cols].astype(F32)
        in_part[step] = total
        in_send[step] = total.astype(BF16)

    def scatter_inner(j, a, b):
        for d in range(1, n_con):
            in_scatter(j, a, b, d).start()

    def reduce_inner(j, a, b):
        group(in_rs.at[:, a:b], in_send_sem.at[0], in_recv_sem.at[0, j]).wait_recv()
        mine = in_part[a:b, share_of(zc)]
        for d in range(1, n_con):
            mine = mine + in_rs[d - 1, a:b].astype(F32)
        in_ag[a:b, share_of(zc)] = mine.astype(BF16)
        for d in range(1, n_con):
            in_gather(j, a, b, d).start()

    solve_y(0, pack - 1)
    for place, (j, a, b) in enumerate(shared):
        steps(max(a, 1), b, solve_y)
        scatter_inner(j, a, b)
        if place:
            reduce_inner(*shared[place - 1])
    if last > 0:
        solve_y(last)
    for d in range(1, n_con):
        in_straight(d).start()
    if shared:
        reduce_inner(*shared[-1])

    group(sq_rs, sq_send_sem.at[1], sq_recv_sem.at[1]).wait_recv()

    def factors(block):
        cols = lanes(block)
        squared = 0.25 + sq_ag[:, cols].astype(F32)
        inverse = lax.rsqrt(squared)
        half = jnp.where(land[:, cols] == 1, -0.5, 0.0)
        ca[:, cols] = half * (squared * inverse)
        cb[:, cols] = half * inverse

    steps(0, n_blk, factors)

    group(send.at[0:n_grid - 1], a2a_send.at[0], a2a_recv.at[0]).wait_send()
    group(sq_rs, sq_send_sem.at[0], sq_recv_sem.at[0]).wait_send()
    group(sq_rs, sq_send_sem.at[1], sq_recv_sem.at[1]).wait_send()
    if shared:
        group(in_rs, in_send_sem.at[0], in_recv_sem.at[0, 0]).wait_send()

    def finish(step, inner):
        cols = lanes(partner(own, step, n_blk))
        first = ca[:, cols]
        second = cb[:, cols] * inner
        for c in range(con_local):
            scaled = w_ref[c] * second
            for p in range(2):
                out_ref[c, p, :, cols] = first * rhs[2 * c + p, :, cols] + scaled * vel[c, p, :, cols].astype(F32)

    def finish_shared(j, a, b):
        group(in_rs.at[:, a:b], in_send_sem.at[1], in_recv_sem.at[1, j]).wait_recv()
        steps(a, b, lambda step: finish(step, in_ag[step].astype(F32)))

    for part in shared[:-1]:
        finish_shared(*part)
    group(in_all, in_send_sem.at[2], in_recv_sem.at[0, 2]).wait_recv()
    total = in_part[last]
    for d in range(1, n_con):
        total = total + in_all[d - 1].astype(F32)
    finish(last, total)
    for part in shared[-1:]:
        finish_shared(*part)
    if shared:
        group(in_rs, in_send_sem.at[1], in_recv_sem.at[0, 0]).wait_send()
    group(in_all, in_send_sem.at[2], in_recv_sem.at[0, 2]).wait_send()


def local(n_con, n_grid, velocity, seed_adjoint, land_mask, inv_x, inv_y, weights):
    con_local, _, rows, side = velocity.shape
    n_blk = inv_x.shape[0]
    pack = BLK // rows
    n_cp = 2 * con_local
    dims = (n_con, n_grid, n_blk, con_local, rows, side)
    share = rows // n_con
    vm = pltpu.VMEM
    sem = pltpu.SemaphoreType.DMA
    peers = max(n_con - 1, 1)
    scratch = [
        vm(velocity.shape, BF16), vm(seed_adjoint.shape, BF16), vm(land_mask.shape, jnp.int32),
        vm(inv_x.shape, BF16), vm(inv_y.shape, BF16), pltpu.SMEM(weights.shape, F32),
        vm((n_grid, rows, n_cp * rows), BF16), vm((n_grid, rows, n_cp * rows), BF16),
        vm((n_blk, pack * BLK, pack * BLK), BF16), vm((n_blk, rows, pack * BLK), BF16),
        vm((rows, side), F32), vm((rows, side), BF16), vm((peers, share, side), BF16), vm((rows, side), BF16),
        vm((n_cp, rows, side), F32), vm((n_blk, rows, BLK), F32), vm((n_blk, rows, BLK), BF16),
        vm((peers, max(n_blk - 1, 1), share, BLK), BF16), vm((n_blk, rows, BLK), BF16),
        vm((peers, rows, BLK), BF16),
        vm((rows, side), F32), vm((rows, side), F32),
        sem((6,)), sem((1,)), sem((n_blk,)), sem((2,)), sem((2,)), sem((3,)), sem((2, 3)),
    ]
    held = sum(math.prod(spec.shape) * jnp.dtype(spec.dtype).itemsize for spec in scratch[:22])
    limit = held + velocity.size * 4 + max(4 << 20, velocity.size * 4)
    anywhere = pl.BlockSpec(memory_space=pltpu.HBM)
    flops = 2 * 2 * n_cp * rows * side * BLK
    return pl.pallas_call(
        functools.partial(kernel, dims),
        out_shape=pltpu.VMEM(velocity.shape, F32),
        in_specs=[anywhere] * 6,
        out_specs=pl.BlockSpec(memory_space=pltpu.VMEM),
        scratch_shapes=scratch,
        cost_estimate=pl.CostEstimate(flops=flops, bytes_accessed=4 * velocity.size * 2, transcendentals=rows * side),
        compiler_params=pltpu.CompilerParams(
            collective_id=0, has_side_effects=True, vmem_limit_bytes=limit),
    )(*(pltpu.with_memory_space_constraint(a, pltpu.HBM) for a in (velocity, seed_adjoint, land_mask, inv_x, inv_y, weights)))


def solution(mesh):
    return jax.shard_map(
        functools.partial(local, mesh.shape["con"], mesh.shape["grid"]),
        mesh=mesh,
        in_specs=(
            P("con", None, "grid", None),
            P("con", None, "grid", None),
            P("grid", None),
            P(),
            P(),
            P("con"),
        ),
        out_specs=P("con", None, "grid", None),
        check_vma=False,
    )
```

```python
import functools
import math
import jax
import jax.numpy as jnp
from jax import lax
from jax.experimental import pallas as pl
from jax.experimental.pallas import tpu as pltpu
from jax.sharding import PartitionSpec as P

BLK = 128
MESH = pl.DeviceIdType.MESH
F32, BF16 = jnp.float32, jnp.bfloat16
LAST = (((1,), (1,)), ((), ()))


def partner(own, step, count):
    if count & (count - 1):
        return lax.rem(own + step, count)
    total, bit = 0, 1
    while bit < count:
        mine = lax.rem(lax.div(own, bit), 2)
        turn = step // bit % 2 if isinstance(step, int) else lax.rem(lax.div(step, bit), 2)
        total = total + lax.rem(mine + turn, 2) * bit
        bit *= 2
    return total


def steps(first, stop, body):
    if stop - first <= 8:
        for step in range(first, stop):
            body(step)
    else:
        @pl.loop(first, stop)
        def _(step):
            body(step)


def lanes(block):
    return pl.ds(pl.multiple_of(block * BLK, BLK), BLK)


def kernel(
    dims,
    vel_hbm, seed_hbm, land_hbm, ix_hbm, iy_hbm, w_hbm,
    out_ref,
    vel, seed, land, ix, iy, w_ref,
    send, recv, wide, mask,
    sq_part, sq_send, sq_rs, sq_ag,
    rhs, in_part, in_send, in_rs, in_ag, in_all, ca, cb,
    load_sem, a2a_send, a2a_recv, sq_send_sem, sq_recv_sem, in_send_sem, in_recv_sem,
):
    n_con, n_grid, n_blk, con_local, rows, side = dims
    pack = BLK // rows
    n_cp = con_local * 2
    groups = n_cp // pack
    share = rows // n_con
    me = lax.axis_index("grid")
    zc = lax.axis_index("con")
    own = lax.div(me, pack)
    core = lax.rem(me, pack)

    loads = []

    def load(src, dst):
        copy = pltpu.make_async_copy(src, dst, load_sem.at[len(loads)])
        copy.start()
        loads.append(copy)

    load(seed_hbm, seed)
    load(ix_hbm, ix)
    barrier = pltpu.get_barrier_semaphore()
    for d in range(1, n_grid):
        pl.semaphore_signal(barrier, inc=1, device_id={"grid": lax.rem(me + d, n_grid)}, device_id_type=MESH)
    for d in range(1, n_con):
        pl.semaphore_signal(barrier, inc=1, device_id={"con": lax.rem(zc + d, n_con)}, device_id_type=MESH)

    load(vel_hbm, vel)
    load(w_hbm, w_ref)
    load(iy_hbm, iy)
    load(land_hbm, land)

    def a2a_copy(peer):
        return pltpu.make_async_remote_copy(
            src_ref=send.at[peer], dst_ref=recv.at[me],
            send_sem=a2a_send.at[0], recv_sem=a2a_recv.at[own],
            device_id={"grid": peer}, device_id_type=MESH)

    def group(ref, send_sem, recv_sem):
        return pltpu.make_async_remote_copy(
            src_ref=ref, dst_ref=ref, send_sem=send_sem, recv_sem=recv_sem,
            device_id={"con": lax.rem(zc + 1, n_con)}, device_id_type=MESH)

    def peer_in(step, slot):
        block = partner(own, step, n_blk)
        return block * pack + slot

    loads[0].wait()
    loads[1].wait()

    def solve_x(step):
        block = partner(own, step, n_blk)
        field = seed[:, :, :, lanes(block)].reshape(n_cp * rows, BLK)
        turned = lax.dot_general(ix[block], field, LAST, preferred_element_type=F32).astype(BF16)
        for half in range(pack):
            send[block * pack + half] = turned[half * rows:(half + 1) * rows]

    pl.semaphore_wait(barrier, n_grid - 1 + n_con - 1)

    def solve_and_send(step):
        solve_x(step)
        for slot in range(pack):
            a2a_copy(peer_in(step, slot)).start()

    steps(1, n_blk, solve_and_send)
    solve_x(0)
    for slot in range(1, pack):
        a2a_copy(own * pack + lax.rem(core + slot, pack)).start()
    recv[me] = send[me]

    loads[2].wait()
    loads[3].wait()

    def square(block):
        cols = lanes(block)
        total = jnp.zeros((rows, BLK), F32)
        for c in range(con_local):
            v0 = vel[c, 0, :, cols].astype(F32)
            v1 = vel[c, 1, :, cols].astype(F32)
            total = total + w_ref[c] * (v0 * v0 + v1 * v1)
        sq_part[:, cols] = total
        sq_send[:, cols] = total.astype(BF16)

    steps(0, n_blk, square)

    def share_of(index):
        return pl.ds(pl.multiple_of(index * share, share), share)

    def sq_scatter(d):
        peer = lax.rem(zc + d, n_con)
        return pltpu.make_async_remote_copy(
            src_ref=sq_send.at[share_of(peer)], dst_ref=sq_rs.at[d - 1],
            send_sem=sq_send_sem.at[0], recv_sem=sq_recv_sem.at[0],
            device_id={"con": peer}, device_id_type=MESH)

    def sq_gather(d):
        peer = lax.rem(zc + d, n_con)
        return pltpu.make_async_remote_copy(
            src_ref=sq_ag.at[share_of(zc)], dst_ref=sq_ag.at[share_of(zc)],
            send_sem=sq_send_sem.at[1], recv_sem=sq_recv_sem.at[1],
            device_id={"con": peer}, device_id_type=MESH)

    for d in range(1, n_con):
        sq_scatter(d).start()

    loads[4].wait()
    loads[5].wait()
    lane = lax.broadcasted_iota(jnp.int32, (BLK, BLK), 1)
    lane_m = lax.broadcasted_iota(jnp.int32, (rows, BLK), 1)

    def spread(tile, lane_of, place, source):
        shift = (place - source) * rows % BLK
        moved = pltpu.roll(tile, shift, 1) if shift else tile
        return jnp.where(lax.div(lane_of, rows) == place, moved, 0.0)

    def prepare(block):
        tile = iy[block].astype(F32)
        sea = (land[:, lanes(block)] == 1).astype(F32)
        for source in range(pack):
            spot = slice(source * BLK, (source + 1) * BLK)
            if pack == 1:
                wide[block] = iy[block]
                mask[block] = sea.astype(BF16)
            else:
                both = jnp.zeros((rows, BLK), F32)
                for place in range(pack):
                    wide[block, place * BLK:(place + 1) * BLK, spot] = spread(tile, lane, place, source).astype(BF16)
                    both = both + spread(sea, lane_m, place, source)
                mask[block, :, spot] = both.astype(BF16)

    steps(0, n_blk, prepare)

    group(sq_rs, sq_send_sem.at[0], sq_recv_sem.at[0]).wait_recv()
    total = sq_part[share_of(zc)]
    for d in range(1, n_con):
        total = total + sq_rs[d - 1].astype(F32)
    sq_ag[share_of(zc)] = total.astype(BF16)
    for d in range(1, n_con):
        sq_gather(d).start()

    last = n_blk - 1
    shared = [(0, 0, last)] if last else []

    def in_scatter(j, a, b, d):
        peer = lax.rem(zc + d, n_con)
        return pltpu.make_async_remote_copy(
            src_ref=in_send.at[a:b, share_of(peer)], dst_ref=in_rs.at[d - 1, a:b],
            send_sem=in_send_sem.at[0], recv_sem=in_recv_sem.at[0, j],
            device_id={"con": peer}, device_id_type=MESH)

    def in_gather(j, a, b, d):
        peer = lax.rem(zc + d, n_con)
        return pltpu.make_async_remote_copy(
            src_ref=in_ag.at[a:b, share_of(zc)], dst_ref=in_ag.at[a:b, share_of(zc)],
            send_sem=in_send_sem.at[1], recv_sem=in_recv_sem.at[1, j],
            device_id={"con": peer}, device_id_type=MESH)

    def in_straight(d):
        peer = lax.rem(zc + d, n_con)
        return pltpu.make_async_remote_copy(
            src_ref=in_send.at[last], dst_ref=in_all.at[d - 1],
            send_sem=in_send_sem.at[2], recv_sem=in_recv_sem.at[0, 2],
            device_id={"con": peer}, device_id_type=MESH)

    def solve_y(step, arriving=pack):
        block = partner(own, step, n_blk)
        if arriving:
            group(recv.at[pl.ds(block * pack, arriving)], a2a_send.at[0], a2a_recv.at[block]).wait_recv()
        cols = lanes(block)
        weight = wide[block]
        keep = mask[block]
        parts = []
        for q in range(groups):
            pieces = [recv[block * pack + source, :, q * BLK:(q + 1) * BLK] for source in range(pack)]
            parts.append((pieces[0] if pack == 1 else jnp.concatenate(pieces, axis=1)) * keep)
        solved = lax.dot_general(jnp.concatenate(parts, axis=0), weight, LAST, preferred_element_type=F32)
        total = jnp.zeros((rows, BLK), F32)
        for cp in range(n_cp):
            q, place = cp // pack, cp % pack
            value = solved[q * rows:(q + 1) * rows, place * BLK:(place + 1) * BLK]
            rhs[cp, :, cols] = value
            total = total + value * vel[cp // 2, cp % 2, :, cols].astype(F32)
        in_part[step] = total
        in_send[step] = total.astype(BF16)

    def scatter_inner(j, a, b):
        for d in range(1, n_con):
            in_scatter(j, a, b, d).start()

    def reduce_inner(j, a, b):
        group(in_rs.at[:, a:b], in_send_sem.at[0], in_recv_sem.at[0, j]).wait_recv()
        mine = in_part[a:b, share_of(zc)]
        for d in range(1, n_con):
            mine = mine + in_rs[d - 1, a:b].astype(F32)
        in_ag[a:b, share_of(zc)] = mine.astype(BF16)
        for d in range(1, n_con):
            in_gather(j, a, b, d).start()

    solve_y(0, pack - 1)
    for place, (j, a, b) in enumerate(shared):
        steps(max(a, 1), b, solve_y)
        scatter_inner(j, a, b)
        if place:
            reduce_inner(*shared[place - 1])
    if last > 0:
        solve_y(last)
    for d in range(1, n_con):
        in_straight(d).start()
    if shared:
        reduce_inner(*shared[-1])

    group(sq_rs, sq_send_sem.at[1], sq_recv_sem.at[1]).wait_recv()

    def factors(block):
        cols = lanes(block)
        squared = 0.25 + sq_ag[:, cols].astype(F32)
        inverse = lax.rsqrt(squared)
        half = jnp.where(land[:, cols] == 1, -0.5, 0.0)
        ca[:, cols] = half * (squared * inverse)
        cb[:, cols] = half * inverse

    steps(0, n_blk, factors)

    group(send.at[0:n_grid - 1], a2a_send.at[0], a2a_recv.at[0]).wait_send()
    group(sq_rs, sq_send_sem.at[0], sq_recv_sem.at[0]).wait_send()
    group(sq_rs, sq_send_sem.at[1], sq_recv_sem.at[1]).wait_send()
    if shared:
        group(in_rs, in_send_sem.at[0], in_recv_sem.at[0, 0]).wait_send()

    def finish(step, inner):
        cols = lanes(partner(own, step, n_blk))
        first = ca[:, cols]
        second = cb[:, cols] * inner
        for c in range(con_local):
            scaled = w_ref[c] * second
            for p in range(2):
                out_ref[c, p, :, cols] = first * rhs[2 * c + p, :, cols] + scaled * vel[c, p, :, cols].astype(F32)

    def finish_shared(j, a, b):
        group(in_rs.at[:, a:b], in_send_sem.at[1], in_recv_sem.at[1, j]).wait_recv()
        steps(a, b, lambda step: finish(step, in_ag[step].astype(F32)))

    group(in_all, in_send_sem.at[2], in_recv_sem.at[0, 2]).wait_recv()
    total = in_part[last]
    for d in range(1, n_con):
        total = total + in_all[d - 1].astype(F32)
    finish(last, total)
    for part in shared:
        finish_shared(*part)
    if shared:
        group(in_rs, in_send_sem.at[1], in_recv_sem.at[0, 0]).wait_send()
    group(in_all, in_send_sem.at[2], in_recv_sem.at[0, 2]).wait_send()


def local(n_con, n_grid, velocity, seed_adjoint, land_mask, inv_x, inv_y, weights):
    con_local, _, rows, side = velocity.shape
    n_blk = inv_x.shape[0]
    pack = BLK // rows
    n_cp = 2 * con_local
    dims = (n_con, n_grid, n_blk, con_local, rows, side)
    share = rows // n_con
    vm = pltpu.VMEM
    sem = pltpu.SemaphoreType.DMA
    peers = max(n_con - 1, 1)
    scratch = [
        vm(velocity.shape, BF16), vm(seed_adjoint.shape, BF16), vm(land_mask.shape, jnp.int32),
        vm(inv_x.shape, BF16), vm(inv_y.shape, BF16), pltpu.SMEM(weights.shape, F32),
        vm((n_grid, rows, n_cp * rows), BF16), vm((n_grid, rows, n_cp * rows), BF16),
        vm((n_blk, pack * BLK, pack * BLK), BF16), vm((n_blk, rows, pack * BLK), BF16),
        vm((rows, side), F32), vm((rows, side), BF16), vm((peers, share, side), BF16), vm((rows, side), BF16),
        vm((n_cp, rows, side), F32), vm((n_blk, rows, BLK), F32), vm((n_blk, rows, BLK), BF16),
        vm((peers, max(n_blk - 1, 1), share, BLK), BF16), vm((n_blk, rows, BLK), BF16),
        vm((peers, rows, BLK), BF16),
        vm((rows, side), F32), vm((rows, side), F32),
        sem((6,)), sem((1,)), sem((n_blk,)), sem((2,)), sem((2,)), sem((3,)), sem((2, 3)),
    ]
    held = sum(math.prod(spec.shape) * jnp.dtype(spec.dtype).itemsize for spec in scratch[:22])
    limit = held + velocity.size * 4 + max(4 << 20, velocity.size * 4)
    anywhere = pl.BlockSpec(memory_space=pltpu.HBM)
    flops = 2 * 2 * n_cp * rows * side * BLK
    return pl.pallas_call(
        functools.partial(kernel, dims),
        out_shape=pltpu.VMEM(velocity.shape, F32),
        in_specs=[anywhere] * 6,
        out_specs=pl.BlockSpec(memory_space=pltpu.VMEM),
        scratch_shapes=scratch,
        cost_estimate=pl.CostEstimate(flops=flops, bytes_accessed=4 * velocity.size * 2, transcendentals=rows * side),
        compiler_params=pltpu.CompilerParams(
            collective_id=0, has_side_effects=True, vmem_limit_bytes=limit),
    )(*(pltpu.with_memory_space_constraint(a, pltpu.HBM) for a in (velocity, seed_adjoint, land_mask, inv_x, inv_y, weights)))


def solution(mesh):
    return jax.shard_map(
        functools.partial(local, mesh.shape["con"], mesh.shape["grid"]),
        mesh=mesh,
        in_specs=(
            P("con", None, "grid", None),
            P("con", None, "grid", None),
            P("grid", None),
            P(),
            P(),
            P("con"),
        ),
        out_specs=P("con", None, "grid", None),
        check_vma=False,
    )
```

```python
import functools
import math
import jax
import jax.numpy as jnp
from jax import lax
from jax.experimental import pallas as pl
from jax.experimental.pallas import tpu as pltpu
from jax.sharding import PartitionSpec as P

BLK = 128
MESH = pl.DeviceIdType.MESH
F32, BF16 = jnp.float32, jnp.bfloat16
LAST = (((1,), (1,)), ((), ()))


def partner(own, step, count):
    if count & (count - 1):
        return lax.rem(own + step, count)
    total, bit = 0, 1
    while bit < count:
        mine = lax.rem(lax.div(own, bit), 2)
        turn = step // bit % 2 if isinstance(step, int) else lax.rem(lax.div(step, bit), 2)
        total = total + lax.rem(mine + turn, 2) * bit
        bit *= 2
    return total


def steps(first, stop, body):
    if stop - first <= 8:
        for step in range(first, stop):
            body(step)
    else:
        @pl.loop(first, stop)
        def _(step):
            body(step)


def lanes(block):
    return pl.ds(pl.multiple_of(block * BLK, BLK), BLK)


def kernel(
    dims,
    vel_hbm, seed_hbm, land_hbm, ix_hbm, iy_hbm, w_hbm,
    out_ref,
    vel, seed, land, ix, iy, w_ref,
    send, recv, wide, mask,
    sq_part, sq_send, sq_rs, sq_ag,
    rhs, in_part, in_send, in_rs, in_ag, ca, cb,
    load_sem, a2a_send, a2a_recv, sq_send_sem, sq_recv_sem, in_send_sem, in_recv_sem,
):
    n_con, n_grid, n_blk, con_local, rows, side = dims
    pack = BLK // rows
    n_cp = con_local * 2
    groups = n_cp // pack
    share = rows // n_con
    me = lax.axis_index("grid")
    zc = lax.axis_index("con")
    own = lax.div(me, pack)
    core = lax.rem(me, pack)

    loads = []

    def load(src, dst):
        copy = pltpu.make_async_copy(src, dst, load_sem.at[len(loads)])
        copy.start()
        loads.append(copy)

    load(seed_hbm, seed)
    load(ix_hbm, ix)
    barrier = pltpu.get_barrier_semaphore()
    for d in range(1, n_grid):
        pl.semaphore_signal(barrier, inc=1, device_id={"grid": lax.rem(me + d, n_grid)}, device_id_type=MESH)
    for d in range(1, n_con):
        pl.semaphore_signal(barrier, inc=1, device_id={"con": lax.rem(zc + d, n_con)}, device_id_type=MESH)

    load(vel_hbm, vel)
    load(w_hbm, w_ref)
    load(iy_hbm, iy)
    load(land_hbm, land)

    def a2a_copy(peer):
        return pltpu.make_async_remote_copy(
            src_ref=send.at[peer], dst_ref=recv.at[me],
            send_sem=a2a_send.at[0], recv_sem=a2a_recv.at[own],
            device_id={"grid": peer}, device_id_type=MESH)

    def group(ref, send_sem, recv_sem):
        return pltpu.make_async_remote_copy(
            src_ref=ref, dst_ref=ref, send_sem=send_sem, recv_sem=recv_sem,
            device_id={"con": lax.rem(zc + 1, n_con)}, device_id_type=MESH)

    def peer_in(step, slot):
        block = partner(own, step, n_blk)
        return block * pack + slot

    loads[0].wait()
    loads[1].wait()

    def solve_x(step):
        block = partner(own, step, n_blk)
        field = seed[:, :, :, lanes(block)].reshape(n_cp * rows, BLK)
        turned = lax.dot_general(ix[block], field, LAST, preferred_element_type=F32).astype(BF16)
        for half in range(pack):
            send[block * pack + half] = turned[half * rows:(half + 1) * rows]

    pl.semaphore_wait(barrier, n_grid - 1 + n_con - 1)

    def solve_and_send(step):
        solve_x(step)
        for slot in range(pack):
            a2a_copy(peer_in(step, slot)).start()

    steps(1, n_blk, solve_and_send)
    solve_x(0)
    for slot in range(1, pack):
        a2a_copy(own * pack + lax.rem(core + slot, pack)).start()
    recv[me] = send[me]

    loads[2].wait()
    loads[3].wait()

    def square(block):
        cols = lanes(block)
        total = jnp.zeros((rows, BLK), F32)
        for c in range(con_local):
            v0 = vel[c, 0, :, cols].astype(F32)
            v1 = vel[c, 1, :, cols].astype(F32)
            total = total + w_ref[c] * (v0 * v0 + v1 * v1)
        sq_part[:, cols] = total
        sq_send[:, cols] = total.astype(BF16)

    steps(0, n_blk, square)

    def share_of(index):
        return pl.ds(pl.multiple_of(index * share, share), share)

    def sq_scatter(d):
        peer = lax.rem(zc + d, n_con)
        return pltpu.make_async_remote_copy(
            src_ref=sq_send.at[share_of(peer)], dst_ref=sq_rs.at[d - 1],
            send_sem=sq_send_sem.at[0], recv_sem=sq_recv_sem.at[0],
            device_id={"con": peer}, device_id_type=MESH)

    def sq_gather(d):
        peer = lax.rem(zc + d, n_con)
        return pltpu.make_async_remote_copy(
            src_ref=sq_ag.at[share_of(zc)], dst_ref=sq_ag.at[share_of(zc)],
            send_sem=sq_send_sem.at[1], recv_sem=sq_recv_sem.at[1],
            device_id={"con": peer}, device_id_type=MESH)

    for d in range(1, n_con):
        sq_scatter(d).start()

    loads[4].wait()
    loads[5].wait()
    lane = lax.broadcasted_iota(jnp.int32, (BLK, BLK), 1)
    lane_m = lax.broadcasted_iota(jnp.int32, (rows, BLK), 1)

    def spread(tile, lane_of, place, source):
        shift = (place - source) * rows % BLK
        moved = pltpu.roll(tile, shift, 1) if shift else tile
        return jnp.where(lax.div(lane_of, rows) == place, moved, 0.0)

    def prepare(block):
        tile = iy[block].astype(F32)
        sea = (land[:, lanes(block)] == 1).astype(F32)
        for source in range(pack):
            spot = slice(source * BLK, (source + 1) * BLK)
            if pack == 1:
                wide[block] = iy[block]
                mask[block] = sea.astype(BF16)
            else:
                both = jnp.zeros((rows, BLK), F32)
                for place in range(pack):
                    wide[block, place * BLK:(place + 1) * BLK, spot] = spread(tile, lane, place, source).astype(BF16)
                    both = both + spread(sea, lane_m, place, source)
                mask[block, :, spot] = both.astype(BF16)

    steps(0, n_blk, prepare)

    def in_scatter(d):
        peer = lax.rem(zc + d, n_con)
        return pltpu.make_async_remote_copy(
            src_ref=in_send.at[:, share_of(peer)], dst_ref=in_rs.at[d - 1],
            send_sem=in_send_sem.at[0], recv_sem=in_recv_sem.at[0],
            device_id={"con": peer}, device_id_type=MESH)

    def in_gather(d):
        peer = lax.rem(zc + d, n_con)
        return pltpu.make_async_remote_copy(
            src_ref=in_ag.at[:, share_of(zc)], dst_ref=in_ag.at[:, share_of(zc)],
            send_sem=in_send_sem.at[1], recv_sem=in_recv_sem.at[1],
            device_id={"con": peer}, device_id_type=MESH)

    def arrive(step, count=pack):
        block = partner(own, step, n_blk)
        group(recv.at[pl.ds(block * pack, count)], a2a_send.at[0], a2a_recv.at[block]).wait_recv()

    def solve_y(step):
        block = partner(own, step, n_blk)
        cols = lanes(block)
        weight = wide[block]
        keep = mask[block]
        parts = []
        for q in range(groups):
            pieces = [recv[block * pack + source, :, q * BLK:(q + 1) * BLK] for source in range(pack)]
            parts.append((pieces[0] if pack == 1 else jnp.concatenate(pieces, axis=1)) * keep)
        solved = lax.dot_general(jnp.concatenate(parts, axis=0), weight, LAST, preferred_element_type=F32)
        total = jnp.zeros((rows, BLK), F32)
        for cp in range(n_cp):
            q, place = cp // pack, cp % pack
            value = solved[q * rows:(q + 1) * rows, place * BLK:(place + 1) * BLK]
            rhs[cp, :, cols] = value
            total = total + value * vel[cp // 2, cp % 2, :, cols].astype(F32)
        in_part[step] = total
        in_send[step] = total.astype(BF16)

    if pack > 1:
        arrive(0, pack - 1)
    solve_y(0)

    group(sq_rs, sq_send_sem.at[0], sq_recv_sem.at[0]).wait_recv()
    total = sq_part[share_of(zc)]
    for d in range(1, n_con):
        total = total + sq_rs[d - 1].astype(F32)
    sq_ag[share_of(zc)] = total.astype(BF16)
    for d in range(1, n_con):
        sq_gather(d).start()

    steps(1, n_blk, arrive)
    steps(1, n_blk, solve_y)
    for d in range(1, n_con):
        in_scatter(d).start()
    group(in_rs, in_send_sem.at[0], in_recv_sem.at[0]).wait_recv()
    mine = in_part[:, share_of(zc)]
    for d in range(1, n_con):
        mine = mine + in_rs[d - 1].astype(F32)
    in_ag[:, share_of(zc)] = mine.astype(BF16)
    for d in range(1, n_con):
        in_gather(d).start()

    group(sq_rs, sq_send_sem.at[1], sq_recv_sem.at[1]).wait_recv()

    def factors(block):
        cols = lanes(block)
        squared = 0.25 + sq_ag[:, cols].astype(F32)
        inverse = lax.rsqrt(squared)
        half = jnp.where(land[:, cols] == 1, -0.5, 0.0)
        ca[:, cols] = half * (squared * inverse)
        cb[:, cols] = half * inverse

    steps(0, n_blk, factors)

    group(send.at[0:n_grid - 1], a2a_send.at[0], a2a_recv.at[0]).wait_send()
    group(sq_rs, sq_send_sem.at[0], sq_recv_sem.at[0]).wait_send()
    group(sq_rs, sq_send_sem.at[1], sq_recv_sem.at[1]).wait_send()
    group(in_rs, in_send_sem.at[0], in_recv_sem.at[0]).wait_send()

    def finish(step):
        cols = lanes(partner(own, step, n_blk))
        first = ca[:, cols]
        second = cb[:, cols] * in_ag[step].astype(F32)
        for c in range(con_local):
            scaled = w_ref[c] * second
            for p in range(2):
                out_ref[c, p, :, cols] = first * rhs[2 * c + p, :, cols] + scaled * vel[c, p, :, cols].astype(F32)

    group(in_rs, in_send_sem.at[1], in_recv_sem.at[1]).wait_recv()
    steps(0, n_blk, finish)
    group(in_rs, in_send_sem.at[1], in_recv_sem.at[1]).wait_send()


def local(n_con, n_grid, velocity, seed_adjoint, land_mask, inv_x, inv_y, weights):
    con_local, _, rows, side = velocity.shape
    n_blk = inv_x.shape[0]
    pack = BLK // rows
    n_cp = 2 * con_local
    dims = (n_con, n_grid, n_blk, con_local, rows, side)
    share = rows // n_con
    vm = pltpu.VMEM
    sem = pltpu.SemaphoreType.DMA
    peers = max(n_con - 1, 1)
    scratch = [
        vm(velocity.shape, BF16), vm(seed_adjoint.shape, BF16), vm(land_mask.shape, jnp.int32),
        vm(inv_x.shape, BF16), vm(inv_y.shape, BF16), pltpu.SMEM(weights.shape, F32),
        vm((n_grid, rows, n_cp * rows), BF16), vm((n_grid, rows, n_cp * rows), BF16),
        vm((n_blk, pack * BLK, pack * BLK), BF16), vm((n_blk, rows, pack * BLK), BF16),
        vm((rows, side), F32), vm((rows, side), BF16), vm((peers, share, side), BF16), vm((rows, side), BF16),
        vm((n_cp, rows, side), F32), vm((n_blk, rows, BLK), F32), vm((n_blk, rows, BLK), BF16),
        vm((peers, n_blk, share, BLK), BF16), vm((n_blk, rows, BLK), BF16),
        vm((rows, side), F32), vm((rows, side), F32),
        sem((6,)), sem((1,)), sem((n_blk,)), sem((2,)), sem((2,)), sem((2,)), sem((2,)),
    ]
    held = sum(math.prod(spec.shape) * jnp.dtype(spec.dtype).itemsize for spec in scratch[:21])
    limit = held + velocity.size * 4 + max(4 << 20, velocity.size * 4)
    anywhere = pl.BlockSpec(memory_space=pltpu.HBM)
    flops = 2 * 2 * n_cp * rows * side * BLK
    return pl.pallas_call(
        functools.partial(kernel, dims),
        out_shape=pltpu.VMEM(velocity.shape, F32),
        in_specs=[anywhere] * 6,
        out_specs=pl.BlockSpec(memory_space=pltpu.VMEM),
        scratch_shapes=scratch,
        cost_estimate=pl.CostEstimate(flops=flops, bytes_accessed=4 * velocity.size * 2, transcendentals=rows * side),
        compiler_params=pltpu.CompilerParams(
            collective_id=0, has_side_effects=True, vmem_limit_bytes=limit),
    )(*(pltpu.with_memory_space_constraint(a, pltpu.HBM) for a in (velocity, seed_adjoint, land_mask, inv_x, inv_y, weights)))


def solution(mesh):
    return jax.shard_map(
        functools.partial(local, mesh.shape["con"], mesh.shape["grid"]),
        mesh=mesh,
        in_specs=(
            P("con", None, "grid", None),
            P("con", None, "grid", None),
            P("grid", None),
            P(),
            P(),
            P("con"),
        ),
        out_specs=P("con", None, "grid", None),
        check_vma=False,
    )
```

```python
import functools
import math
import jax
import jax.numpy as jnp
from jax import lax
from jax.experimental import pallas as pl
from jax.experimental.pallas import tpu as pltpu
from jax.sharding import PartitionSpec as P

BLK = 128
MESH = pl.DeviceIdType.MESH
F32, BF16 = jnp.float32, jnp.bfloat16
LAST = (((1,), (1,)), ((), ()))


def partner(own, step, count):
    if count & (count - 1):
        return lax.rem(own + step, count)
    total, bit = 0, 1
    while bit < count:
        mine = lax.rem(lax.div(own, bit), 2)
        turn = step // bit % 2 if isinstance(step, int) else lax.rem(lax.div(step, bit), 2)
        total = total + lax.rem(mine + turn, 2) * bit
        bit *= 2
    return total


def steps(first, stop, body):
    if stop - first <= 1:
        for step in range(first, stop):
            body(step)
    else:
        @pl.loop(first, stop)
        def _(step):
            body(step)


def lanes(block):
    return pl.ds(pl.multiple_of(block * BLK, BLK), BLK)


def kernel(
    dims,
    vel_hbm, seed_hbm, land_hbm, ix_hbm, iy_hbm, w_hbm,
    out_ref,
    vel, seed, land, ix, iy, w_ref,
    send, recv, wide, mask,
    sq_part, sq_send, sq_rs, sq_ag,
    rhs, in_part, in_send, in_rs, in_ag, in_all, ca, cb,
    load_sem, a2a_send, a2a_recv, sq_send_sem, sq_recv_sem, in_send_sem, in_recv_sem,
):
    n_con, n_grid, n_blk, con_local, rows, side = dims
    pack = BLK // rows
    n_cp = con_local * 2
    groups = n_cp // pack
    share = rows // n_con
    me = lax.axis_index("grid")
    zc = lax.axis_index("con")
    own = lax.div(me, pack)
    core = lax.rem(me, pack)

    loads = []

    def load(src, dst):
        copy = pltpu.make_async_copy(src, dst, load_sem.at[len(loads)])
        copy.start()
        loads.append(copy)

    load(seed_hbm, seed)
    load(ix_hbm, ix)
    barrier = pltpu.get_barrier_semaphore()
    for d in range(1, n_grid):
        pl.semaphore_signal(barrier, inc=1, device_id={"grid": lax.rem(me + d, n_grid)}, device_id_type=MESH)
    for d in range(1, n_con):
        pl.semaphore_signal(barrier, inc=1, device_id={"con": lax.rem(zc + d, n_con)}, device_id_type=MESH)

    load(vel_hbm, vel)
    load(w_hbm, w_ref)
    load(iy_hbm, iy)
    load(land_hbm, land)

    def a2a_copy(peer):
        return pltpu.make_async_remote_copy(
            src_ref=send.at[peer], dst_ref=recv.at[me],
            send_sem=a2a_send.at[0], recv_sem=a2a_recv.at[own],
            device_id={"grid": peer}, device_id_type=MESH)

    def group(ref, send_sem, recv_sem):
        return pltpu.make_async_remote_copy(
            src_ref=ref, dst_ref=ref, send_sem=send_sem, recv_sem=recv_sem,
            device_id={"con": lax.rem(zc + 1, n_con)}, device_id_type=MESH)

    def peer_in(step, slot):
        block = partner(own, step, n_blk)
        return block * pack + slot

    loads[0].wait()
    loads[1].wait()

    def solve_x(step):
        block = partner(own, step, n_blk)
        field = seed[:, :, :, lanes(block)].reshape(n_cp * rows, BLK)
        turned = lax.dot_general(ix[block], field, LAST, preferred_element_type=F32).astype(BF16)
        for half in range(pack):
            send[block * pack + half] = turned[half * rows:(half + 1) * rows]

    pl.semaphore_wait(barrier, n_grid - 1 + n_con - 1)

    def solve_and_send(step):
        solve_x(step)
        for slot in range(pack):
            a2a_copy(peer_in(step, slot)).start()

    steps(1, n_blk, solve_and_send)
    solve_x(0)
    for slot in range(1, pack):
        a2a_copy(own * pack + lax.rem(core + slot, pack)).start()
    recv[me] = send[me]

    loads[2].wait()
    loads[3].wait()

    def square(block):
        cols = lanes(block)
        total = jnp.zeros((rows, BLK), F32)
        for c in range(con_local):
            v0 = vel[c, 0, :, cols].astype(F32)
            v1 = vel[c, 1, :, cols].astype(F32)
            total = total + w_ref[c] * (v0 * v0 + v1 * v1)
        sq_part[:, cols] = total
        sq_send[:, cols] = total.astype(BF16)

    steps(0, n_blk, square)

    def share_of(index):
        return pl.ds(pl.multiple_of(index * share, share), share)

    def sq_scatter(d):
        peer = lax.rem(zc + d, n_con)
        return pltpu.make_async_remote_copy(
            src_ref=sq_send.at[share_of(peer)], dst_ref=sq_rs.at[d - 1],
            send_sem=sq_send_sem.at[0], recv_sem=sq_recv_sem.at[0],
            device_id={"con": peer}, device_id_type=MESH)

    def sq_gather(d):
        peer = lax.rem(zc + d, n_con)
        return pltpu.make_async_remote_copy(
            src_ref=sq_ag.at[share_of(zc)], dst_ref=sq_ag.at[share_of(zc)],
            send_sem=sq_send_sem.at[1], recv_sem=sq_recv_sem.at[1],
            device_id={"con": peer}, device_id_type=MESH)

    for d in range(1, n_con):
        sq_scatter(d).start()

    loads[4].wait()
    loads[5].wait()
    lane = lax.broadcasted_iota(jnp.int32, (BLK, BLK), 1)
    lane_m = lax.broadcasted_iota(jnp.int32, (rows, BLK), 1)

    def spread(tile, lane_of, place, source):
        shift = (place - source) * rows % BLK
        moved = pltpu.roll(tile, shift, 1) if shift else tile
        return jnp.where(lax.div(lane_of, rows) == place, moved, 0.0)

    def prepare(block):
        tile = iy[block].astype(F32)
        sea = (land[:, lanes(block)] == 1).astype(F32)
        for source in range(pack):
            spot = slice(source * BLK, (source + 1) * BLK)
            if pack == 1:
                wide[block] = iy[block]
                mask[block] = sea.astype(BF16)
            else:
                both = jnp.zeros((rows, BLK), F32)
                for place in range(pack):
                    wide[block, place * BLK:(place + 1) * BLK, spot] = spread(tile, lane, place, source).astype(BF16)
                    both = both + spread(sea, lane_m, place, source)
                mask[block, :, spot] = both.astype(BF16)

    steps(0, n_blk, prepare)

    group(sq_rs, sq_send_sem.at[0], sq_recv_sem.at[0]).wait_recv()
    total = sq_part[share_of(zc)]
    for d in range(1, n_con):
        total = total + sq_rs[d - 1].astype(F32)
    sq_ag[share_of(zc)] = total.astype(BF16)
    for d in range(1, n_con):
        sq_gather(d).start()

    last = n_blk - 1
    shared = [(0, 0, last)] if last else []

    def in_scatter(j, a, b, d):
        peer = lax.rem(zc + d, n_con)
        return pltpu.make_async_remote_copy(
            src_ref=in_send.at[a:b, share_of(peer)], dst_ref=in_rs.at[d - 1, a:b],
            send_sem=in_send_sem.at[0], recv_sem=in_recv_sem.at[0, j],
            device_id={"con": peer}, device_id_type=MESH)

    def in_gather(j, a, b, d):
        peer = lax.rem(zc + d, n_con)
        return pltpu.make_async_remote_copy(
            src_ref=in_ag.at[a:b, share_of(zc)], dst_ref=in_ag.at[a:b, share_of(zc)],
            send_sem=in_send_sem.at[1], recv_sem=in_recv_sem.at[1, j],
            device_id={"con": peer}, device_id_type=MESH)

    def in_straight(d):
        peer = lax.rem(zc + d, n_con)
        return pltpu.make_async_remote_copy(
            src_ref=in_send.at[last], dst_ref=in_all.at[d - 1],
            send_sem=in_send_sem.at[2], recv_sem=in_recv_sem.at[0, 2],
            device_id={"con": peer}, device_id_type=MESH)

    def solve_y(step, arriving=pack):
        block = partner(own, step, n_blk)
        if arriving:
            group(recv.at[pl.ds(block * pack, arriving)], a2a_send.at[0], a2a_recv.at[block]).wait_recv()
        cols = lanes(block)
        weight = wide[block]
        keep = mask[block]
        parts = []
        for q in range(groups):
            pieces = [recv[block * pack + source, :, q * BLK:(q + 1) * BLK] for source in range(pack)]
            parts.append((pieces[0] if pack == 1 else jnp.concatenate(pieces, axis=1)) * keep)
        solved = lax.dot_general(jnp.concatenate(parts, axis=0), weight, LAST, preferred_element_type=F32)
        total = jnp.zeros((rows, BLK), F32)
        for cp in range(n_cp):
            q, place = cp // pack, cp % pack
            value = solved[q * rows:(q + 1) * rows, place * BLK:(place + 1) * BLK]
            rhs[cp, :, cols] = value
            total = total + value * vel[cp // 2, cp % 2, :, cols].astype(F32)
        in_part[step] = total
        in_send[step] = total.astype(BF16)

    def scatter_inner(j, a, b):
        for d in range(1, n_con):
            in_scatter(j, a, b, d).start()

    def reduce_inner(j, a, b):
        group(in_rs.at[:, a:b], in_send_sem.at[0], in_recv_sem.at[0, j]).wait_recv()
        mine = in_part[a:b, share_of(zc)]
        for d in range(1, n_con):
            mine = mine + in_rs[d - 1, a:b].astype(F32)
        in_ag[a:b, share_of(zc)] = mine.astype(BF16)
        for d in range(1, n_con):
            in_gather(j, a, b, d).start()

    solve_y(0, pack - 1)
    for place, (j, a, b) in enumerate(shared):
        steps(max(a, 1), b, solve_y)
        scatter_inner(j, a, b)
        if place:
            reduce_inner(*shared[place - 1])
    if last > 0:
        solve_y(last)
    for d in range(1, n_con):
        in_straight(d).start()
    if shared:
        reduce_inner(*shared[-1])

    group(sq_rs, sq_send_sem.at[1], sq_recv_sem.at[1]).wait_recv()

    def factors(block):
        cols = lanes(block)
        squared = 0.25 + sq_ag[:, cols].astype(F32)
        inverse = lax.rsqrt(squared)
        half = jnp.where(land[:, cols] == 1, -0.5, 0.0)
        ca[:, cols] = half * (squared * inverse)
        cb[:, cols] = half * inverse

    steps(0, n_blk, factors)

    group(send.at[0:n_grid - 1], a2a_send.at[0], a2a_recv.at[0]).wait_send()
    group(sq_rs, sq_send_sem.at[0], sq_recv_sem.at[0]).wait_send()
    group(sq_rs, sq_send_sem.at[1], sq_recv_sem.at[1]).wait_send()
    if shared:
        group(in_rs, in_send_sem.at[0], in_recv_sem.at[0, 0]).wait_send()

    def finish(step, inner):
        cols = lanes(partner(own, step, n_blk))
        first = ca[:, cols]
        second = cb[:, cols] * inner
        for c in range(con_local):
            scaled = w_ref[c] * second
            for p in range(2):
                out_ref[c, p, :, cols] = first * rhs[2 * c + p, :, cols] + scaled * vel[c, p, :, cols].astype(F32)

    def finish_shared(j, a, b):
        group(in_rs.at[:, a:b], in_send_sem.at[1], in_recv_sem.at[1, j]).wait_recv()
        steps(a, b, lambda step: finish(step, in_ag[step].astype(F32)))

    group(in_all, in_send_sem.at[2], in_recv_sem.at[0, 2]).wait_recv()
    total = in_part[last]
    for d in range(1, n_con):
        total = total + in_all[d - 1].astype(F32)
    finish(last, total)
    for part in shared:
        finish_shared(*part)
    if shared:
        group(in_rs, in_send_sem.at[1], in_recv_sem.at[0, 0]).wait_send()
    group(in_all, in_send_sem.at[2], in_recv_sem.at[0, 2]).wait_send()


def local(n_con, n_grid, velocity, seed_adjoint, land_mask, inv_x, inv_y, weights):
    con_local, _, rows, side = velocity.shape
    n_blk = inv_x.shape[0]
    pack = BLK // rows
    n_cp = 2 * con_local
    dims = (n_con, n_grid, n_blk, con_local, rows, side)
    share = rows // n_con
    vm = pltpu.VMEM
    sem = pltpu.SemaphoreType.DMA
    peers = max(n_con - 1, 1)
    scratch = [
        vm(velocity.shape, BF16), vm(seed_adjoint.shape, BF16), vm(land_mask.shape, jnp.int32),
        vm(inv_x.shape, BF16), vm(inv_y.shape, BF16), pltpu.SMEM(weights.shape, F32),
        vm((n_grid, rows, n_cp * rows), BF16), vm((n_grid, rows, n_cp * rows), BF16),
        vm((n_blk, pack * BLK, pack * BLK), BF16), vm((n_blk, rows, pack * BLK), BF16),
        vm((rows, side), F32), vm((rows, side), BF16), vm((peers, share, side), BF16), vm((rows, side), BF16),
        vm((n_cp, rows, side), F32), vm((n_blk, rows, BLK), F32), vm((n_blk, rows, BLK), BF16),
        vm((peers, max(n_blk - 1, 1), share, BLK), BF16), vm((n_blk, rows, BLK), BF16),
        vm((peers, rows, BLK), BF16),
        vm((rows, side), F32), vm((rows, side), F32),
        sem((6,)), sem((1,)), sem((n_blk,)), sem((2,)), sem((2,)), sem((3,)), sem((2, 3)),
    ]
    held = sum(math.prod(spec.shape) * jnp.dtype(spec.dtype).itemsize for spec in scratch[:22])
    limit = held + velocity.size * 4 + max(4 << 20, velocity.size * 4)
    anywhere = pl.BlockSpec(memory_space=pltpu.HBM)
    flops = 2 * 2 * n_cp * rows * side * BLK
    return pl.pallas_call(
        functools.partial(kernel, dims),
        out_shape=pltpu.VMEM(velocity.shape, F32),
        in_specs=[anywhere] * 6,
        out_specs=pl.BlockSpec(memory_space=pltpu.VMEM),
        scratch_shapes=scratch,
        cost_estimate=pl.CostEstimate(flops=flops, bytes_accessed=4 * velocity.size * 2, transcendentals=rows * side),
        compiler_params=pltpu.CompilerParams(
            collective_id=0, has_side_effects=True, vmem_limit_bytes=limit),
    )(*(pltpu.with_memory_space_constraint(a, pltpu.HBM) for a in (velocity, seed_adjoint, land_mask, inv_x, inv_y, weights)))


def solution(mesh):
    return jax.shard_map(
        functools.partial(local, mesh.shape["con"], mesh.shape["grid"]),
        mesh=mesh,
        in_specs=(
            P("con", None, "grid", None),
            P("con", None, "grid", None),
            P("grid", None),
            P(),
            P(),
            P("con"),
        ),
        out_specs=P("con", None, "grid", None),
        check_vma=False,
    )
```
